512 devices in a mesh: loop: 64 (over y_hi, z, core), grp: 8 (over x, y_lo).
Axes of the slice: x: 4, y: 4 (y_hi: 2, y_lo: 2; y = y_hi * 2 + y_lo), z: 16, core: 2. Of those that a mesh axis runs over, the one named last changes fastest.
Arguments:
- student: bfloat16 [65536, 1024], P('loop', 'grp'), may hold values from -0.75 to 0.75
- teacher_tiles: bfloat16 [65536, 4, 1024], P(('loop', 'grp')), may hold values from -0.59765625 to 0.59765625
Outputs:
- student_grad: float32 [65536, 1024], P('loop', 'grp')
The draws below stay inside these ranges and needn't reach their ends.
All inputs are finite; a program needn't handle non-finite values.
Results may differ from the reference program's by a relative error of at most 0.0052.
Values may be sent and summed in bfloat16 or wider, within the bound.
A program may use at most 64 MiB of HBM per device.

```python
import math
import jax
import jax.numpy as jnp
from jax import lax

DS = 1024
BLK = 1024
STEPS = 4
TOKENS = 65536
N_LOOP = 64


def draw_student(key, part):
    key = jax.random.fold_in(key, 11)
    base_key, row_key, col_key = jax.random.split(key, 3)
    base = jnp.clip(jax.random.normal(base_key, (TOKENS, DS), jnp.float32), -4.0, 4.0)
    row_scale = jnp.exp(jax.random.uniform(row_key, (TOKENS, 1), jnp.float32, 0.0, math.log(10.0)))
    col_scale = jnp.exp(jax.random.uniform(col_key, (1, DS), jnp.float32, 0.0, math.log(3.0)))
    return (base * row_scale * col_scale / 160.0).astype(jnp.bfloat16)


def level_of(own_key, extent, shards, least, top_value):
    gain = 1.0
    for dim, shards_of in shards:
        draws = jax.random.uniform(jax.random.fold_in(jax.random.fold_in(own_key, 6), dim), (shards_of,), jnp.float32, least / len(shards), top_value / len(shards))
        gain = gain * jnp.repeat(jnp.exp(draws), extent[dim] // shards_of).reshape((-1,) + (1,) * (len(extent) - 1 - dim))
    return gain


def gaussian(rng, dims, scale, reach, cuts=(), dtype=jnp.bfloat16):
    array = scale * jax.random.normal(rng, dims, jnp.float32)
    if cuts:
        array = array * level_of(rng, dims, cuts, -0.22, 0.18)
    return jnp.clip(array, -reach, reach).astype(dtype)


def setup_inputs(seed: int = 0) -> dict:
    seeds = jax.random.split(jax.random.key(seed), 3)
    return {
        "student": draw_student(jax.random.fold_in(seeds[2], 71), 0),
        "teacher_tiles": gaussian(seeds[1], (TOKENS, STEPS, BLK), 0.1, 0.59765625, ((0, 512),)),
    }


def reference(student, teacher_tiles):
    values = student.astype(jnp.float32)
    norms = jnp.sqrt(lax.optimization_barrier(jnp.sum(values * values, axis=1)) + 1e-06)
    unit = values / norms[:, None]
    unit_bf = unit.astype(jnp.bfloat16)
    blocks = unit_bf.reshape(N_LOOP, BLK, DS).astype(jnp.float32)
    tiles = teacher_tiles.reshape(N_LOOP, BLK, STEPS, BLK)
    own_grad = jnp.zeros((N_LOOP, BLK, DS), jnp.float32)
    far_grad = jnp.zeros((N_LOOP, BLK, DS), jnp.float32)
    for step in range(STEPS):
        visitor = jnp.roll(blocks, step, axis=0)
        similar = jnp.einsum('nrd,ncd->nrc', blocks, visitor)
        errors = (similar - tiles[:, :, step, :].astype(jnp.float32)).astype(jnp.bfloat16).astype(jnp.float32)
        own_grad = own_grad + jnp.einsum('nrc,ncd->nrd', errors, visitor)
        far_term = jnp.einsum('nrc,nrd->ncd', errors, blocks)
        far_grad = far_grad + jnp.roll(far_term, -step, axis=0)
    unit_grad = (2.0 * own_grad + 2.0 * far_grad).reshape(N_LOOP * BLK, DS)
    inner = lax.optimization_barrier(jnp.sum(unit * unit_grad, axis=1))
    return (unit_grad - unit * inner[:, None]) / norms[:, None]
```

```python
import functools

import jax
import jax.numpy as jnp
from jax import lax
from jax.experimental import pallas as pl
from jax.experimental.pallas import tpu as pltpu
from jax.sharding import PartitionSpec as P

MESH = pl.DeviceIdType.MESH
F32 = jnp.float32
BF16 = jnp.bfloat16
STEPS = 4


def to_lanes(column, eye):
    return jnp.sum(jnp.where(eye, column, 0.0), axis=0, keepdims=True)


def to_column(row, eye):
    return jnp.sum(jnp.where(eye, row, 0.0), axis=1, keepdims=True)


def kernel(
    n_loop, n_grp, s_ref, t_ref, out_ref,
    raw, unit, norm, rows_raw, rows_norm, urows, tiles, errors, own_send, own_recv, far_send, far_recv,
    own_total, own_rows, home_rows, inner_send, inner_recv,
    early_s, early_r, gather_s, gather_r, tile_s, tile_r, unit_s, unit_r, own_s, own_r, far_s, far_r,
    rows_s, rows_r, inner_s, inner_r,
):
    b = lax.axis_index("loop")
    g = lax.axis_index("grp")
    rows, width = s_ref.shape
    feats = width * n_grp
    part = rows // n_grp

    def mate(d):
        return lax.rem(g + 1 + d, n_grp)

    def below(k):
        return (lax.rem(b + n_loop - k, n_loop), g)

    def above(k):
        return (lax.rem(b + k, n_loop), g)

    def lanes(h, n=width):
        return pl.ds(pl.multiple_of(h * width, width), n)

    def part_of(h):
        return pl.ds(pl.multiple_of(h * part, part), part)

    def send(src, dst, s, r, to):
        copy = pltpu.make_async_remote_copy(
            src_ref=src, dst_ref=dst, send_sem=s, recv_sem=r, device_id=to, device_id_type=MESH
        )
        copy.start()
        return copy

    barrier = pltpu.get_barrier_semaphore()
    for d in range(n_grp - 1):
        pl.semaphore_signal(barrier, inc=1, device_id=(b, mate(d)), device_id_type=MESH)
    for k in range(1, STEPS):
        pl.semaphore_signal(barrier, inc=1, device_id=below(k), device_id_type=MESH)
        pl.semaphore_signal(barrier, inc=1, device_id=above(k), device_id_type=MESH)
    pl.semaphore_wait(barrier, n_grp - 1 + 2 * (STEPS - 1))

    early = [
        send(s_ref.at[part_of(mate(d)), :], rows_raw.at[:, lanes(g)], early_s.at[d], early_r.at[d], (b, mate(d)))
        for d in range(n_grp - 1)
    ]
    tile_copies = [
        send(t_ref.at[k], tiles.at[k - 1], tile_s.at[k - 1], tile_r.at[k - 1], below(k)) for k in range(1, STEPS)
    ]
    gather = [
        send(s_ref, raw.at[:, lanes(g)], gather_s.at[d], gather_r.at[d], (b, mate(d))) for d in range(n_grp - 1)
    ]
    raw[:, lanes(g)] = s_ref[...]
    rows_raw[:, lanes(g)] = s_ref[part_of(g), :]

    for copy in early:
        copy.wait_recv()
    values = rows_raw[...].astype(F32)
    row_norms = jnp.sqrt(jnp.sum(values * values, axis=1, keepdims=True) + 1e-06)
    rows_norm[...] = row_norms
    urows[0] = (values / row_norms).astype(BF16)
    unit_copies = [
        send(urows.at[0], urows.at[k], unit_s.at[k - 1], unit_r.at[k - 1], below(k)) for k in range(1, STEPS)
    ]

    for copy in gather:
        copy.wait_recv()

    def normalise(i, carry):
        at = pl.ds(pl.multiple_of(i * part, part), part)
        values = raw[at, :].astype(F32)
        norms = jnp.sqrt(jnp.sum(values * values, axis=1, keepdims=True) + 1e-06)
        norm[at, :] = norms
        unit[at, :] = (values / norms).astype(BF16)
        return carry

    lax.fori_loop(0, n_grp, normalise, 0)

    def error_tile(k, tile):
        mine = urows[k]

        def chunk(i, carry):
            at = pl.ds(pl.multiple_of(i * 256, 256), 256)
            similar = lax.dot_general(mine, unit[at, :], (((1,), (1,)), ((), ())), preferred_element_type=F32)
            errors[pl.ds(k * part, part), at] = (similar - tile[:, at].astype(F32)).astype(BF16)
            return carry

        lax.fori_loop(0, rows // 256, chunk, 0)

    def own_part(k, store):
        def chunk(i, carry):
            at = pl.ds(pl.multiple_of(i * 256, 256), 256)
            store(at, jnp.dot(errors[pl.ds(k * part, part), :], unit[:, at], preferred_element_type=F32))
            return carry

        lax.fori_loop(0, feats // 256, chunk, 0)

    def keep(at, value):
        own_total[:, at] = value

    error_tile(0, t_ref.at[0])
    own_part(0, keep)
    own_copies = []
    for k in range(1, STEPS):
        unit_copies[k - 1].wait_recv()
        tile_copies[k - 1].wait_recv()
        error_tile(k, tiles.at[k - 1])

        def put(at, value, k=k):
            own_send[k - 1, :, at] = value.astype(BF16)

        own_part(k, put)
        own_copies.append(
            send(own_send.at[k - 1], own_recv.at[k - 1], own_s.at[k - 1], own_r.at[k - 1], above(k))
        )

    far_copies = []
    for i in range(n_grp // 2):
        pair = lax.rem(lax.div(g, 2) + 1 + i, n_grp // 2)
        at = pl.ds(pl.multiple_of(pair * 2 * width, 2 * width), 2 * width)
        for j in range(STEPS):
            piece = lax.dot_general(
                errors[:, pl.ds(j * rows // STEPS, rows // STEPS)],
                urows[:, :, at].reshape(STEPS * part, 2 * width),
                (((0,), (0,)), ((), ())),
                preferred_element_type=F32,
            )
            far_send[pl.ds(j * rows // STEPS, rows // STEPS), at] = piece.astype(BF16)
        here = [pair * 2, pair * 2 + 1] if i < n_grp // 2 - 1 else [g + 1 - 2 * lax.rem(g, 2)]
        for h in here:
            n = len(far_copies)
            slot = lax.rem(g - h + n_grp + n_grp - 1, n_grp)
            far_copies.append(
                send(far_send.at[:, lanes(h)], far_recv.at[slot], far_s.at[n], far_r.at[slot], (b, h))
            )

    eye = lax.broadcasted_iota(jnp.int32, (part, part), 0) == lax.broadcasted_iota(jnp.int32, (part, part), 1)

    def inner_rows(i, carry):
        at = pl.ds(pl.multiple_of(i * part, part), part)
        dots = jnp.sum(raw[at, :].astype(F32) * far_send[at, :].astype(F32), axis=1, keepdims=True)
        inner_send[pl.ds(i, 1), :] = to_lanes(dots / norm[at, :], eye)
        return carry

    lax.fori_loop(0, n_grp, inner_rows, 0)

    for copy in own_copies:
        copy.wait_recv()
    total = own_total[...]
    for k in range(1, STEPS):
        total = total + own_recv[k - 1].astype(F32)
    rounded = total.astype(BF16)
    own_rows[...] = rounded
    rows_copies = [
        send(own_rows.at[:, lanes(mate(d))], home_rows.at[part_of(g), :], rows_s.at[d], rows_r.at[d], (b, mate(d)))
        for d in range(n_grp - 1)
    ]
    dots = jnp.sum(rows_raw[...].astype(F32) * rounded.astype(F32), axis=1, keepdims=True)
    inner_send[pl.ds(g, 1), :] = inner_send[pl.ds(g, 1), :] + to_lanes(dots / rows_norm[...], eye)
    inner_copies = [
        send(inner_send, inner_recv.at[d], inner_s.at[d], inner_r.at[d], (b, mate(d))) for d in range(n_grp - 1)
    ]
    home_rows[part_of(g), :] = own_rows[:, lanes(g)]

    for copy in rows_copies + inner_copies + far_copies:
        copy.wait_recv()

    inner = inner_send[...]
    for d in range(n_grp - 1):
        inner = inner + inner_recv[d]

    for i in range(n_grp):
        at = pl.ds(i * part, part)
        grad = home_rows[at, :].astype(F32) + far_send[at, lanes(g)].astype(F32)
        for d in range(n_grp - 1):
            grad = grad + far_recv[d, at, :].astype(F32)
        norms = norm[at, :]
        along = to_column(inner[i : i + 1, :], eye)
        out_ref[at, :] = 2.0 * (grad - (s_ref[at, :].astype(F32) / norms) * along) / norms

    for copy in early + tile_copies + gather + unit_copies + own_copies + far_copies + rows_copies + inner_copies:
        copy.wait_send()


def per_device(n_loop, n_grp, student, teacher_tiles):
    rows, width = student.shape
    feats = width * n_grp
    part = rows // n_grp
    mates, hops = n_grp - 1, STEPS - 1
    tiles = jnp.transpose(teacher_tiles, (1, 0, 2))
    dma = pltpu.SemaphoreType.DMA
    scratch = [
        pltpu.VMEM((rows, feats), BF16),
        pltpu.VMEM((rows, feats), BF16),
        pltpu.VMEM((rows, 1), F32),
        pltpu.VMEM((part, feats), BF16),
        pltpu.VMEM((part, 1), F32),
        pltpu.VMEM((STEPS, part, feats), BF16),
        pltpu.VMEM((hops, part, rows), BF16),
        pltpu.VMEM((STEPS * part, rows), BF16),
        pltpu.VMEM((hops, part, feats), BF16),
        pltpu.VMEM((hops, part, feats), BF16),
        pltpu.VMEM((rows, feats), BF16),
        pltpu.VMEM((mates, rows, width), BF16),
        pltpu.VMEM((part, feats), F32),
        pltpu.VMEM((part, feats), BF16),
        pltpu.VMEM((rows, width), BF16),
        pltpu.VMEM((n_grp, part), F32),
        pltpu.VMEM((mates, n_grp, part), F32),
    ]
    for count in (mates, mates, hops, hops, hops, mates, mates, mates):
        scratch += [dma((count,)), dma((count,))]
    return pl.pallas_call(
        functools.partial(kernel, n_loop, n_grp),
        out_shape=jax.ShapeDtypeStruct((rows, width), F32),
        in_specs=[pl.BlockSpec(memory_space=pltpu.VMEM)] * 2,
        out_specs=pl.BlockSpec(memory_space=pltpu.VMEM),
        scratch_shapes=scratch,
        compiler_params=pltpu.CompilerParams(
            collective_id=0, has_side_effects=True, vmem_limit_bytes=56 * 2**20
        ),
        name="window_grad",
    )(student, tiles)


def solution(mesh):
    placed = (P("loop", "grp"), P(("loop", "grp"), None, None))
    return jax.shard_map(
        functools.partial(per_device, mesh.shape["loop"], mesh.shape["grp"]),
        mesh=mesh, in_specs=placed, out_specs=P("loop", "grp"), check_vma=False,
    )
```

```python
import functools

import jax
import jax.numpy as jnp
from jax import lax
from jax.experimental import pallas as pl
from jax.experimental.pallas import tpu as pltpu
from jax.sharding import PartitionSpec as P

MESH = pl.DeviceIdType.MESH
F32 = jnp.float32
BF16 = jnp.bfloat16
STEPS = 4
HALVES = 2
G_SIDE, G_LEFT, G_LEFT_SIDE, G_RIGHT, G_RIGHT_SIDE, G_LEFT_FAR, G_RIGHT_FAR = range(7)
R_LEFT_PASS, R_RIGHT_PASS, R_LEFT, R_RIGHT, R_LEFT_SUM, R_RIGHT_SUM, R_SIDE = range(7)


def to_lanes(column, eye):
    return jnp.sum(jnp.where(eye, column, 0.0), axis=0, keepdims=True)


def to_column(row, eye):
    return jnp.sum(jnp.where(eye, row, 0.0), axis=1, keepdims=True)


def kernel(
    n_loop, n_grp, s_ref, t_ref, out_ref,
    raw, unit, squares, norm, rows_raw, rows_norm, urows, tiles, errors, own_send, own_recv,
    far, landed, passed, side, own_total, own_rows, home_rows, inner_send, inner_recv,
    early_s, early_r, gather_s, gather_r, tile_s, tile_r, unit_s, unit_r, own_s, own_r, far_s, far_r,
    rows_s, rows_r, inner_s, inner_r,
):
    b = lax.axis_index("loop")
    g = lax.axis_index("grp")
    rows, width = s_ref.shape
    feats = width * n_grp
    part = rows // n_grp
    half = rows // HALVES
    n_x = n_grp // 2
    x, y = lax.div(g, 2), lax.rem(g, 2)

    def at_x(dx, other=False):
        return lax.rem(x + dx + n_x, n_x) * 2 + (1 - y if other else y)

    def mate(d):
        return lax.rem(g + 1 + d, n_grp)

    def below(k):
        return (lax.rem(b + n_loop - k, n_loop), g)

    def above(k):
        return (lax.rem(b + k, n_loop), g)

    def part_of(h):
        return pl.ds(pl.multiple_of(h * part, part), part)

    started = []

    def send(src, dst, s, r, to):
        copy = pltpu.make_async_remote_copy(
            src_ref=src, dst_ref=dst, send_sem=s, recv_sem=r, device_id=to, device_id_type=MESH
        )
        copy.start()
        started.append(copy)
        return copy

    right, left, beside = (b, at_x(1)), (b, at_x(-1)), (b, at_x(0, True))

    barrier = pltpu.get_barrier_semaphore()
    for d in range(n_grp - 1):
        pl.semaphore_signal(barrier, inc=1, device_id=(b, mate(d)), device_id_type=MESH)
    for k in range(1, STEPS):
        pl.semaphore_signal(barrier, inc=1, device_id=below(k), device_id_type=MESH)
        pl.semaphore_signal(barrier, inc=1, device_id=above(k), device_id_type=MESH)
    pl.semaphore_wait(barrier, n_grp - 1 + 2 * (STEPS - 1))

    early = [
        send(s_ref.at[part_of(mate(d)), :], rows_raw.at[g], early_s.at[d], early_r.at[d], (b, mate(d)))
        for d in range(n_grp - 1)
    ]
    sent_slices = []

    def give(src, h, slot, to):
        n = len(sent_slices)
        sent_slices.append(send(src, raw.at[h], gather_s.at[n], gather_r.at[slot], to))

    def take(slot):
        pltpu.make_async_copy(raw.at[0], raw.at[0], gather_r.at[slot]).wait()

    give(s_ref, g, G_SIDE, beside)
    give(s_ref, g, G_LEFT, right)
    give(s_ref, g, G_RIGHT, left)

    def send_tile(k):
        return send(t_ref.at[k], tiles.at[k - 1], tile_s.at[k - 1], tile_r.at[k - 1], below(k))

    def send_unit(k):
        return send(urows.at[k], urows.at[k + 1], unit_s.at[k], unit_r.at[k], below(1))

    tile_copies = {3: send_tile(3)}
    raw[g] = s_ref[...]
    rows_raw[g] = s_ref[part_of(g), :]

    def add_squares(h, first=False):
        def block(i, carry):
            at = pl.ds(pl.multiple_of(i * part, part), part)
            values = raw[h, at, :].astype(F32)
            squares[at, :] = values * values if first else squares[at, :] + values * values
            return carry

        lax.fori_loop(0, n_grp, block, 0)

    for copy in early:
        copy.wait_recv()
    total = jnp.zeros((part, width), F32)
    for h in range(n_grp):
        values = rows_raw[h].astype(F32)
        total = total + values * values
    norms = jnp.sqrt(jnp.sum(total, axis=1, keepdims=True) + 1e-06)
    rows_norm[...] = norms
    for h in range(n_grp):
        urows[0, :, h * width : (h + 1) * width] = (rows_raw[h].astype(F32) / norms).astype(BF16)
    unit_copies = [send_unit(0)]
    tile_copies[2] = send_tile(2)
    add_squares(g, first=True)

    take(G_SIDE)
    give(raw.at[at_x(0, True)], at_x(0, True), G_LEFT_SIDE, right)
    take(G_LEFT)
    give(raw.at[at_x(-1)], at_x(-1), G_LEFT_FAR, right)
    give(raw.at[at_x(0, True)], at_x(0, True), G_RIGHT_SIDE, left)
    add_squares(at_x(0, True))
    add_squares(at_x(-1))
    unit_copies[0].wait_recv()
    unit_copies.append(send_unit(1))
    tile_copies[1] = send_tile(1)
    take(G_RIGHT)
    add_squares(at_x(1))
    take(G_RIGHT_SIDE)
    give(raw.at[at_x(1, True)], at_x(1, True), G_RIGHT_FAR, left)
    add_squares(at_x(1, True))
    unit_copies[1].wait_recv()
    unit_copies.append(send_unit(2))
    take(G_LEFT_SIDE)
    add_squares(at_x(-1, True))
    take(G_LEFT_FAR)
    add_squares(at_x(-2))
    take(G_RIGHT_FAR)
    add_squares(at_x(2, True))

    def normalise(i, carry):
        at = pl.ds(pl.multiple_of(i * part, part), part)
        norms = jnp.sqrt(jnp.sum(squares[at, :], axis=1, keepdims=True) + 1e-06)
        norm[at, :] = norms
        inverse = 1.0 / norms
        for h in range(n_grp):
            unit[at, h * width : (h + 1) * width] = (raw[h, at, :].astype(F32) * inverse).astype(BF16)
        return carry

    lax.fori_loop(0, n_grp, normalise, 0)

    def error_tile(k, tile):
        mine = urows[k]

        def chunk(i, carry):
            at = pl.ds(pl.multiple_of(i * 256, 256), 256)
            similar = lax.dot_general(mine, unit[at, :], (((1,), (1,)), ((), ())), preferred_element_type=F32)
            errors[pl.ds(k * part, part), at] = (similar - tile[:, at].astype(F32)).astype(BF16)
            return carry

        lax.fori_loop(0, rows // 256, chunk, 0)

    def own_part(k, store):
        def chunk(i, carry):
            at = pl.ds(pl.multiple_of(i * 256, 256), 256)
            store(at, jnp.dot(errors[pl.ds(k * part, part), :], unit[:, at], preferred_element_type=F32))
            return carry

        lax.fori_loop(0, feats // 256, chunk, 0)

    def keep(at, value):
        own_total[:, at] = value

    error_tile(0, t_ref.at[0])
    own_part(0, keep)
    own_copies = []
    for k in range(1, STEPS):
        if k == STEPS - 1:
            unit_copies[k - 1].wait_recv()
        tile_copies[k].wait_recv()
        error_tile(k, tiles.at[k - 1])

        def put(at, value, k=k):
            own_send[k - 1, :, at] = value.astype(BF16)

        own_part(k, put)
        own_copies.append(
            send(own_send.at[k - 1], own_recv.at[k - 1], own_s.at[k - 1], own_r.at[k - 1], above(k))
        )

    def far_pair(dx):
        pair = lax.rem(x + dx + n_x, n_x)
        mine = urows[:, :, pl.ds(pl.multiple_of(pair * 2 * width, 2 * width), 2 * width)].reshape(
            STEPS * part, 2 * width
        )

        def chunk(i, carry):
            at = pl.ds(pl.multiple_of(i * 256, 256), 256)
            piece = lax.dot_general(
                errors[:, at], mine, (((0,), (0,)), ((), ())), preferred_element_type=F32
            ).astype(BF16)
            far[pair * 2, at, :] = piece[:, :width]
            far[pair * 2 + 1, at, :] = piece[:, width:]
            return carry

        lax.fori_loop(0, rows // 256, chunk, 0)

    sent_sums = []

    def hand(src, slot, to, i=None):
        n = len(sent_sums)
        dst, r = landed.at[slot], far_r.at[slot, 0]
        if i is not None:
            src, dst, r = src.at[pl.ds(i * half, half), :], dst.at[pl.ds(i * half, half), :], far_r.at[slot, i]
        sent_sums.append(send(src, dst, far_s.at[n], r, to))

    def got(slot, i=None):
        at = pl.ds(0, rows) if i is None else pl.ds(i * half, half)
        here = landed.at[slot, at, :]
        pltpu.make_async_copy(here, here, far_r.at[slot, i or 0]).wait()

    far_pair(2)
    hand(far.at[at_x(2, True)], R_LEFT_PASS, right)
    hand(far.at[at_x(2)], R_RIGHT_PASS, left)
    far_pair(1)
    hand(far.at[at_x(1)], R_LEFT, right)
    far_pair(-1)
    hand(far.at[at_x(-1, True)], R_RIGHT, left)
    far_pair(0)

    eye = lax.broadcasted_iota(jnp.int32, (part, part), 0) == lax.broadcasted_iota(jnp.int32, (part, part), 1)

    def inner_rows(i, carry):
        at = pl.ds(pl.multiple_of(i * part, part), part)
        dots = jnp.zeros((part, width), F32)
        for h in range(n_grp):
            dots = dots + raw[h, at, :].astype(F32) * far[h, at, :].astype(F32)
        inner_send[pl.ds(i, 1), :] = to_lanes(jnp.sum(dots, axis=1, keepdims=True) / norm[at, :], eye)
        return carry

    lax.fori_loop(0, n_grp, inner_rows, 0)

    got(R_LEFT_PASS)
    got(R_RIGHT_PASS)
    for i in range(HALVES):
        at = pl.ds(i * half, half)
        passed[0, at, :] = (far[at_x(1, True), at, :].astype(F32) + landed[R_LEFT_PASS, at, :].astype(F32)).astype(BF16)
        hand(passed.at[0], R_LEFT_SUM, right, i)
        passed[1, at, :] = (far[at_x(-1), at, :].astype(F32) + landed[R_RIGHT_PASS, at, :].astype(F32)).astype(BF16)
        hand(passed.at[1], R_RIGHT_SUM, left, i)

    for copy in own_copies:
        copy.wait_recv()
    total = own_total[...]
    for k in range(1, STEPS):
        total = total + own_recv[k - 1].astype(F32)
    dots = jnp.zeros((part, width), F32)
    for h in range(n_grp):
        rounded = total[:, h * width : (h + 1) * width].astype(BF16)
        own_rows[h] = rounded
        dots = dots + rows_raw[h].astype(F32) * rounded.astype(F32)
    rows_copies = [
        send(own_rows.at[mate(d)], home_rows.at[part_of(g), :], rows_s.at[d], rows_r.at[d], (b, mate(d)))
        for d in range(n_grp - 1)
    ]
    inner_send[pl.ds(g, 1), :] = inner_send[pl.ds(g, 1), :] + to_lanes(
        jnp.sum(dots, axis=1, keepdims=True) / rows_norm[...], eye
    )
    inner_copies = [
        send(inner_send, inner_recv.at[d], inner_s.at[d], inner_r.at[d], (b, mate(d))) for d in range(n_grp - 1)
    ]
    home_rows[part_of(g), :] = own_rows[g]

    got(R_LEFT)
    got(R_RIGHT)
    for i in range(HALVES):
        at = pl.ds(i * half, half)
        got(R_LEFT_SUM, i)
        side[at, :] = (
            far[at_x(0, True), at, :].astype(F32)
            + landed[R_RIGHT, at, :].astype(F32)
            + landed[R_LEFT_SUM, at, :].astype(F32)
        ).astype(BF16)
        hand(side, R_SIDE, beside, i)

    for copy in rows_copies + inner_copies:
        copy.wait_recv()
    inner = inner_send[...]
    for d in range(n_grp - 1):
        inner = inner + inner_recv[d]

    for i in range(n_grp):
        if i % (n_grp // HALVES) == 0:
            got(R_RIGHT_SUM, i // (n_grp // HALVES))
            got(R_SIDE, i // (n_grp // HALVES))
        at = pl.ds(i * part, part)
        grad = home_rows[at, :].astype(F32) + far[g, at, :].astype(F32)
        for slot in (R_LEFT, R_RIGHT_SUM, R_SIDE):
            grad = grad + landed[slot, at, :].astype(F32)
        norms = norm[at, :]
        along = to_column(inner[i : i + 1, :], eye)
        out_ref[at, :] = 2.0 * (grad - (s_ref[at, :].astype(F32) / norms) * along) / norms

    for copy in started:
        copy.wait_send()


def per_device(n_loop, n_grp, student, teacher_tiles):
    rows, width = student.shape
    feats = width * n_grp
    part = rows // n_grp
    mates, hops = n_grp - 1, STEPS - 1
    tiles = jnp.transpose(teacher_tiles, (1, 0, 2))
    dma = pltpu.SemaphoreType.DMA
    scratch = [
        pltpu.VMEM((n_grp, rows, width), BF16),
        pltpu.VMEM((rows, feats), BF16),
        pltpu.VMEM((rows, width), F32),
        pltpu.VMEM((rows, 1), F32),
        pltpu.VMEM((n_grp, part, width), BF16),
        pltpu.VMEM((part, 1), F32),
        pltpu.VMEM((STEPS, part, feats), BF16),
        pltpu.VMEM((hops, part, rows), BF16),
        pltpu.VMEM((STEPS * part, rows), BF16),
        pltpu.VMEM((hops, part, feats), BF16),
        pltpu.VMEM((hops, part, feats), BF16),
        pltpu.VMEM((n_grp, rows, width), BF16),
        pltpu.VMEM((7, rows, width), BF16),
        pltpu.VMEM((2, rows, width), BF16),
        pltpu.VMEM((rows, width), BF16),
        pltpu.VMEM((part, feats), F32),
        pltpu.VMEM((n_grp, part, width), BF16),
        pltpu.VMEM((rows, width), BF16),
        pltpu.VMEM((n_grp, part), F32),
        pltpu.VMEM((mates, n_grp, part), F32),
        dma((mates,)), dma((mates,)),
        dma((7,)), dma((7,)),
        dma((hops,)), dma((hops,)),
        dma((hops,)), dma((hops,)),
        dma((hops,)), dma((hops,)),
        dma((4 + 3 * HALVES,)), dma((7, HALVES)),
        dma((mates,)), dma((mates,)),
        dma((mates,)), dma((mates,)),
    ]
    return pl.pallas_call(
        functools.partial(kernel, n_loop, n_grp),
        out_shape=jax.ShapeDtypeStruct((rows, width), F32),
        in_specs=[pl.BlockSpec(memory_space=pltpu.VMEM)] * 2,
        out_specs=pl.BlockSpec(memory_space=pltpu.VMEM),
        scratch_shapes=scratch,
        compiler_params=pltpu.CompilerParams(
            collective_id=0, has_side_effects=True, vmem_limit_bytes=56 * 2**20
        ),
        name="window_grad",
    )(student, tiles)


def solution(mesh):
    placed = (P("loop", "grp"), P(("loop", "grp"), None, None))
    return jax.shard_map(
        functools.partial(per_device, mesh.shape["loop"], mesh.shape["grp"]),
        mesh=mesh, in_specs=placed, out_specs=P("loop", "grp"), check_vma=False,
    )
```

```python
import functools

import jax
import jax.numpy as jnp
from jax import lax
from jax.experimental import pallas as pl
from jax.experimental.pallas import tpu as pltpu
from jax.sharding import PartitionSpec as P

MESH = pl.DeviceIdType.MESH
F32 = jnp.float32
BF16 = jnp.bfloat16
STEPS = 4
HALVES = 2
G_SIDE, G_LEFT, G_LEFT_SIDE, G_RIGHT, G_RIGHT_SIDE, G_LEFT_FAR, G_RIGHT_FAR = range(7)
R_LEFT_PASS, R_RIGHT_PASS, R_LEFT, R_RIGHT, R_LEFT_SUM, R_RIGHT_SUM, R_SIDE = range(7)


def to_lanes(column, eye):
    return jnp.sum(jnp.where(eye, column, 0.0), axis=0, keepdims=True)


def to_column(row, eye):
    return jnp.sum(jnp.where(eye, row, 0.0), axis=1, keepdims=True)


def kernel(
    n_loop, n_grp, s_ref, t_ref, out_ref,
    raw, unit, squares, norm, rows_raw, rows_norm, urows, sent_tiles, tiles, third, errors, errors_t, own_send, own_recv,
    far, landed, passed, side, own_total, own_rows, home_rows, inner_send, inner_recv,
    early_s, early_r, gather_s, gather_r, tile_s, tile_r, third_s, third_r, unit_s, unit_r, own_s, own_r, far_s, far_r,
    rows_s, rows_r, inner_s, inner_r,
):
    b = lax.axis_index("loop")
    g = lax.axis_index("grp")
    rows, width = s_ref.shape
    feats = width * n_grp
    part = rows // n_grp
    half = rows // HALVES
    step = min(256, half)
    n_x = n_grp // 2
    x, y = lax.div(g, 2), lax.rem(g, 2)

    def at_x(dx, other=False):
        return lax.rem(x + dx + n_x, n_x) * 2 + (1 - y if other else y)

    def mate(d):
        return lax.rem(g + 1 + d, n_grp)

    def block(k):
        return (lax.rem(b + n_loop + k, n_loop), g)

    def part_of(h):
        return pl.ds(pl.multiple_of(h * part, part), part)

    def half_of(i):
        return pl.ds(i * half, half)

    started = []

    def send(src, dst, s, r, to):
        copy = pltpu.make_async_remote_copy(
            src_ref=src, dst_ref=dst, send_sem=s, recv_sem=r, device_id=to, device_id_type=MESH
        )
        copy.start()
        started.append(copy)
        return copy

    right, left, beside = (b, at_x(1)), (b, at_x(-1)), (b, at_x(0, True))

    barrier = pltpu.get_barrier_semaphore()
    for d in range(n_grp - 1):
        pl.semaphore_signal(barrier, inc=1, device_id=(b, mate(d)), device_id_type=MESH)
    for k in range(1, STEPS):
        pl.semaphore_signal(barrier, inc=1, device_id=block(-k), device_id_type=MESH)
        pl.semaphore_signal(barrier, inc=1, device_id=block(k), device_id_type=MESH)

    tiles[pl.ds(0, part), :] = t_ref[:, 0, :]
    for k in range(1, STEPS - 1):
        sent_tiles[k - 1] = t_ref[:, k, :]
    last = t_ref[:, STEPS - 1, :]
    for h in range(n_grp):
        third[0, h] = last[:, h * part : (h + 1) * part]
    raw[g] = s_ref[...]
    rows_raw[g] = s_ref[part_of(g), :]

    def add_squares(h, i, first=False):
        def piece(j, carry):
            at = pl.ds(pl.multiple_of(i * half + j * part, part), part)
            values = raw[h, at, :].astype(F32)
            squares[at, :] = values * values if first else squares[at, :] + values * values
            return carry

        lax.fori_loop(0, half // part, piece, 0)

    for i in range(HALVES):
        add_squares(g, i, first=True)

    pl.semaphore_wait(barrier, n_grp - 1 + 2 * (STEPS - 1))

    early = [
        send(s_ref.at[part_of(mate(d)), :], rows_raw.at[g], early_s.at[d], early_r.at[d], (b, mate(d)))
        for d in range(n_grp - 1)
    ]
    sent_slices = []

    def give(h, i, slot, to, src=None):
        n = len(sent_slices)
        src = raw.at[h] if src is None else src
        sent_slices.append(
            send(src.at[half_of(i), :], raw.at[h, half_of(i), :], gather_s.at[n], gather_r.at[slot, i], to)
        )

    def take(slot, h, i):
        here = raw.at[h, half_of(i), :]
        pltpu.make_async_copy(here, here, gather_r.at[slot, i]).wait()

    for i in range(HALVES):
        give(g, i, G_SIDE, beside, s_ref)
        give(g, i, G_LEFT, right, s_ref)
        give(g, i, G_RIGHT, left, s_ref)

    def send_tile(k):
        dst = tiles.at[pl.ds(k * part, part), :]
        return send(sent_tiles.at[k - 1], dst, tile_s.at[k - 1], tile_r.at[k - 1], block(-k))

    def urow(k):
        return urows.at[pl.ds(k * part, part), :]

    tile_copies = [send_tile(2), send_tile(1)]
    third_copies = [
        send(third.at[0, mate(d)], third.at[1, g], third_s.at[d], third_r.at[d], (b, mate(d)))
        for d in range(n_grp - 1)
    ]
    third[1, g] = third[0, g]

    for copy in early:
        copy.wait_recv()
    total = jnp.zeros((part, width), F32)
    for h in range(n_grp):
        values = rows_raw[h].astype(F32)
        total = total + values * values
    norms = jnp.sqrt(jnp.sum(total, axis=1, keepdims=True) + 1e-06)
    rows_norm[...] = norms
    for h in range(n_grp):
        urows[0:part, h * width : (h + 1) * width] = (rows_raw[h].astype(F32) / norms).astype(BF16)
    unit_copies = [
        send(urow(0), urow(1), unit_s.at[0], unit_r.at[0], block(-1)),
        send(urow(0), urow(3), unit_s.at[2], unit_r.at[2], block(3)),
    ]

    def pass_on(i):
        take(G_SIDE, at_x(0, True), i)
        give(at_x(0, True), i, G_LEFT_SIDE, right)
        give(at_x(0, True), i, G_RIGHT_SIDE, left)
        take(G_LEFT, at_x(-1), i)
        give(at_x(-1), i, G_LEFT_FAR, right)

    def pass_back(i):
        take(G_RIGHT_SIDE, at_x(1, True), i)
        give(at_x(1, True), i, G_RIGHT_FAR, left)

    def use(i, *slices):
        for h in slices:
            add_squares(h, i)

    pass_on(0)
    use(0, at_x(0, True), at_x(-1))
    unit_copies[0].wait_recv()
    unit_copies.append(send(urow(1), urow(2), unit_s.at[1], unit_r.at[1], block(-1)))
    pass_on(1)
    pass_back(0)
    use(0, at_x(1, True))
    take(G_RIGHT, at_x(1), 0)
    take(G_LEFT_SIDE, at_x(-1, True), 0)
    use(0, at_x(1), at_x(-1, True))
    take(G_LEFT_FAR, at_x(-2), 0)
    use(0, at_x(-2))
    use(1, at_x(0, True), at_x(-1))
    for copy in third_copies:
        copy.wait_recv()
    for h in range(n_grp):
        tiles[3 * part : 4 * part, h * part : (h + 1) * part] = third[1, h].astype(F32).T.astype(BF16)
    take(G_RIGHT_FAR, at_x(2, True), 0)
    use(0, at_x(2, True))
    pass_back(1)

    def normalise(i):
        def piece(j, carry):
            at = pl.ds(pl.multiple_of(i * half + j * part, part), part)
            norms = jnp.sqrt(jnp.sum(squares[at, :], axis=1, keepdims=True) + 1e-06)
            norm[at, :] = norms
            inverse = 1.0 / norms
            for h in range(n_grp):
                unit[at, h * width : (h + 1) * width] = (raw[h, at, :].astype(F32) * inverse).astype(BF16)
            return carry

        lax.fori_loop(0, half // part, piece, 0)

    def error_tiles(i):
        def piece(j, carry):
            at = pl.ds(pl.multiple_of(i * half + j * step, step), step)
            similar = lax.dot_general(
                urows[...], unit[at, :], (((1,), (1,)), ((), ())), preferred_element_type=F32
            )
            found = similar - tiles[:, at].astype(F32)
            errors[:, at] = found.astype(BF16)
            errors_t[at, :] = found.T.astype(BF16)
            return carry

        lax.fori_loop(0, half // step, piece, 0)

    def far_pair(dx, i):
        pair = lax.rem(x + dx + n_x, n_x)
        mine = urows[:, pl.ds(pl.multiple_of(pair * 2 * width, 2 * width), 2 * width)]

        def piece(j, carry):
            at = pl.ds(pl.multiple_of(i * half + j * step, step), step)
            sums = jnp.dot(errors_t[at, :], mine, preferred_element_type=F32).astype(BF16)
            far[pair * 2, at, :] = sums[:, :width]
            far[pair * 2 + 1, at, :] = sums[:, width:]
            return carry

        lax.fori_loop(0, half // step, piece, 0)

    sent_sums = []

    def hand(src, i, slot, to):
        n = len(sent_sums)
        sent_sums.append(
            send(src.at[half_of(i), :], landed.at[slot, half_of(i), :], far_s.at[n], far_r.at[slot, i], to)
        )

    def got(slot, i):
        here = landed.at[slot, half_of(i), :]
        pltpu.make_async_copy(here, here, far_r.at[slot, i]).wait()

    def far_terms(i):
        far_pair(2, i)
        hand(far.at[at_x(2, True)], i, R_LEFT_PASS, right)
        hand(far.at[at_x(2)], i, R_RIGHT_PASS, left)
        far_pair(1, i)
        hand(far.at[at_x(1)], i, R_LEFT, right)
        far_pair(-1, i)
        hand(far.at[at_x(-1, True)], i, R_RIGHT, left)
        far_pair(0, i)

    def add_passed(i):
        at = half_of(i)
        got(R_LEFT_PASS, i)
        passed[0, at, :] = (far[at_x(1, True), at, :].astype(F32) + landed[R_LEFT_PASS, at, :].astype(F32)).astype(BF16)
        hand(passed.at[0], i, R_LEFT_SUM, right)
        got(R_RIGHT_PASS, i)
        passed[1, at, :] = (far[at_x(-1), at, :].astype(F32) + landed[R_RIGHT_PASS, at, :].astype(F32)).astype(BF16)
        hand(passed.at[1], i, R_RIGHT_SUM, left)

    def add_side(i):
        at = half_of(i)
        got(R_RIGHT, i)
        got(R_LEFT_SUM, i)
        side[at, :] = (
            far[at_x(0, True), at, :].astype(F32)
            + landed[R_RIGHT, at, :].astype(F32)
            + landed[R_LEFT_SUM, at, :].astype(F32)
        ).astype(BF16)
        hand(side, i, R_SIDE, beside)

    for copy in tile_copies + unit_copies[1:]:
        copy.wait_recv()
    normalise(0)
    error_tiles(0)
    far_terms(0)

    use(1, at_x(1, True))
    take(G_RIGHT, at_x(1), 1)
    take(G_LEFT_SIDE, at_x(-1, True), 1)
    use(1, at_x(1), at_x(-1, True))
    take(G_LEFT_FAR, at_x(-2), 1)
    take(G_RIGHT_FAR, at_x(2, True), 1)
    use(1, at_x(-2), at_x(2, True))
    normalise(1)
    error_tiles(1)

    def own_parts(j, carry):
        at = pl.ds(pl.multiple_of(j * 256, 256), 256)
        found = jnp.dot(errors[...], unit[:, at], preferred_element_type=F32)
        own_total[:, at] = found[:part]
        for k in range(1, STEPS):
            own_send[k - 1, :, at] = found[k * part : (k + 1) * part].astype(BF16)
        return carry

    lax.fori_loop(0, feats // 256, own_parts, 0)
    own_copies = [
        send(own_send.at[k - 1], own_recv.at[k - 1], own_s.at[k - 1], own_r.at[k - 1], block(k if k < 3 else -3))
        for k in range(1, STEPS)
    ]
    far_terms(1)
    add_passed(0)

    eye = lax.broadcasted_iota(jnp.int32, (part, part), 0) == lax.broadcasted_iota(jnp.int32, (part, part), 1)

    def inner_rows(i, carry):
        at = pl.ds(pl.multiple_of(i * part, part), part)
        dots = jnp.zeros((part, width), F32)
        for h in range(n_grp):
            dots = dots + raw[h, at, :].astype(F32) * far[h, at, :].astype(F32)
        inner_send[pl.ds(i, 1), :] = to_lanes(jnp.sum(dots, axis=1, keepdims=True) / norm[at, :], eye)
        return carry

    lax.fori_loop(0, n_grp, inner_rows, 0)
    add_passed(1)

    for copy in own_copies:
        copy.wait_recv()
    total = own_total[...]
    for k in range(1, STEPS):
        total = total + own_recv[k - 1].astype(F32)
    dots = jnp.zeros((part, width), F32)
    for h in range(n_grp):
        rounded = total[:, h * width : (h + 1) * width].astype(BF16)
        own_rows[h] = rounded
        dots = dots + rows_raw[h].astype(F32) * rounded.astype(F32)
    rows_copies = [
        send(own_rows.at[mate(d)], home_rows.at[part_of(g), :], rows_s.at[d], rows_r.at[d], (b, mate(d)))
        for d in range(n_grp - 1)
    ]
    inner_send[pl.ds(g, 1), :] = inner_send[pl.ds(g, 1), :] + to_lanes(
        jnp.sum(dots, axis=1, keepdims=True) / rows_norm[...], eye
    )
    inner_copies = [
        send(inner_send, inner_recv.at[d], inner_s.at[d], inner_r.at[d], (b, mate(d))) for d in range(n_grp - 1)
    ]
    home_rows[part_of(g), :] = own_rows[g]

    for i in range(HALVES):
        add_side(i)

    for copy in rows_copies + inner_copies:
        copy.wait_recv()
    inner = inner_send[...]
    for d in range(n_grp - 1):
        inner = inner + inner_recv[d]

    for i in range(n_grp):
        if i % (n_grp // HALVES) == 0:
            for slot in (R_LEFT, R_RIGHT_SUM, R_SIDE):
                got(slot, i // (n_grp // HALVES))
        at = pl.ds(i * part, part)
        grad = home_rows[at, :].astype(F32) + far[g, at, :].astype(F32)
        for slot in (R_LEFT, R_RIGHT_SUM, R_SIDE):
            grad = grad + landed[slot, at, :].astype(F32)
        inverse = 1.0 / norm[at, :]
        along = to_column(inner[i : i + 1, :], eye)
        out_ref[at, :] = (2.0 * inverse) * (grad - s_ref[at, :].astype(F32) * (inverse * along))

    for copy in started:
        copy.wait_send()


def per_device(n_loop, n_grp, student, teacher_tiles):
    rows, width = student.shape
    feats = width * n_grp
    part = rows // n_grp
    mates, hops = n_grp - 1, STEPS - 1
    dma = pltpu.SemaphoreType.DMA
    scratch = [
        pltpu.VMEM((n_grp, rows, width), BF16),
        pltpu.VMEM((rows, feats), BF16),
        pltpu.VMEM((rows, width), F32),
        pltpu.VMEM((rows, 1), F32),
        pltpu.VMEM((n_grp, part, width), BF16),
        pltpu.VMEM((part, 1), F32),
        pltpu.VMEM((STEPS * part, feats), BF16),
        pltpu.VMEM((hops - 1, part, rows), BF16),
        pltpu.VMEM((STEPS * part, rows), BF16),
        pltpu.VMEM((2, n_grp, part, part), BF16),
        pltpu.VMEM((STEPS * part, rows), BF16),
        pltpu.VMEM((rows, STEPS * part), BF16),
        pltpu.VMEM((hops, part, feats), BF16),
        pltpu.VMEM((hops, part, feats), BF16),
        pltpu.VMEM((n_grp, rows, width), BF16),
        pltpu.VMEM((7, rows, width), BF16),
        pltpu.VMEM((2, rows, width), BF16),
        pltpu.VMEM((rows, width), BF16),
        pltpu.VMEM((part, feats), F32),
        pltpu.VMEM((n_grp, part, width), BF16),
        pltpu.VMEM((rows, width), BF16),
        pltpu.VMEM((n_grp, part), F32),
        pltpu.VMEM((mates, n_grp, part), F32),
        dma((mates,)), dma((mates,)),
        dma((7 * HALVES,)), dma((7, HALVES)),
        dma((hops - 1,)), dma((hops - 1,)),
        dma((mates,)), dma((mates,)),
        dma((hops,)), dma((hops,)),
        dma((hops,)), dma((hops,)),
        dma((7 * HALVES,)), dma((7, HALVES)),
        dma((mates,)), dma((mates,)),
        dma((mates,)), dma((mates,)),
    ]
    return pl.pallas_call(
        functools.partial(kernel, n_loop, n_grp),
        out_shape=jax.ShapeDtypeStruct((rows, width), F32),
        in_specs=[pl.BlockSpec(memory_space=pltpu.VMEM)] * 2,
        out_specs=pl.BlockSpec(memory_space=pltpu.VMEM),
        scratch_shapes=scratch,
        compiler_params=pltpu.CompilerParams(
            collective_id=0, has_side_effects=True, vmem_limit_bytes=56 * 2**20
        ),
        name="window_grad",
    )(student, teacher_tiles)


def solution(mesh):
    placed = (P("loop", "grp"), P(("loop", "grp"), None, None))
    return jax.shard_map(
        functools.partial(per_device, mesh.shape["loop"], mesh.shape["grp"]),
        mesh=mesh, in_specs=placed, out_specs=P("loop", "grp"), check_vma=False,
    )
```

```python
import functools

import jax
import jax.numpy as jnp
from jax import lax
from jax.experimental import pallas as pl
from jax.experimental.pallas import tpu as pltpu
from jax.sharding import PartitionSpec as P

MESH = pl.DeviceIdType.MESH
F32 = jnp.float32
BF16 = jnp.bfloat16
STEPS = 4
HALVES = 2
G_SIDE, G_LEFT, G_LEFT_SIDE, G_RIGHT, G_RIGHT_SIDE, G_LEFT_FAR, G_RIGHT_FAR = range(7)
R_LEFT_PASS, R_RIGHT_PASS, R_LEFT, R_RIGHT, R_LEFT_SUM, R_RIGHT_SUM, R_SIDE = range(7)


def to_lanes(column, eye):
    return jnp.sum(jnp.where(eye, column, 0.0), axis=0, keepdims=True)


def to_column(row, eye):
    return jnp.sum(jnp.where(eye, row, 0.0), axis=1, keepdims=True)


def kernel(
    n_loop, n_grp, s_ref, t_ref, out_ref,
    raw, unit, squares, norm, rows_raw, rows_norm, urows, sent_tiles, tiles, third, errors, errors_t, own_send, own_recv,
    far, landed, passed, side, own_total, own_rows, home_rows, inner_send, inner_recv,
    below_in, early_s, early_r, gather_s, gather_r, tile_s, tile_r, third_s, third_r, unit_s, unit_r, own_s, own_r, far_s, far_r,
    rows_s, rows_r, inner_s, inner_r,
):
    b = lax.axis_index("loop")
    g = lax.axis_index("grp")
    rows, width = s_ref.shape
    feats = width * n_grp
    part = rows // n_grp
    half = rows // HALVES
    step = half
    n_x = n_grp // 2
    x, y = lax.div(g, 2), lax.rem(g, 2)

    def at_x(dx, other=False):
        return lax.rem(x + dx + n_x, n_x) * 2 + (1 - y if other else y)

    def mate(d):
        return lax.rem(g + 1 + d, n_grp)

    def block(k):
        return (lax.rem(b + n_loop + k, n_loop), g)

    def part_of(h):
        return pl.ds(pl.multiple_of(h * part, part), part)

    def half_of(i):
        return pl.ds(i * half, half)

    def features(c):
        first = 1 - lax.div(g, n_grp // 2)
        return pl.ds(pl.multiple_of((first if c == 0 else 1 - first) * (feats // 2), feats // 2), feats // 2)

    started = []

    def send(src, dst, s, r, to):
        copy = pltpu.make_async_remote_copy(
            src_ref=src, dst_ref=dst, send_sem=s, recv_sem=r, device_id=to, device_id_type=MESH
        )
        copy.start()
        started.append(copy)
        return copy

    right, left, beside = (b, at_x(1)), (b, at_x(-1)), (b, at_x(0, True))

    barrier = pltpu.get_barrier_semaphore()
    for d in range(n_grp - 1):
        pl.semaphore_signal(barrier, inc=1, device_id=(b, mate(d)), device_id_type=MESH)
    for k in range(1, STEPS):
        pl.semaphore_signal(barrier, inc=1, device_id=block(-k), device_id_type=MESH)

    tiles[pl.ds(0, part), :] = t_ref[:, 0, :]
    for k in range(1, STEPS - 1):
        sent_tiles[k - 1] = t_ref[:, k, :]
    last = t_ref[:, STEPS - 1, :]
    for h in range(n_grp):
        third[0, h] = last[:, h * part : (h + 1) * part]
    raw[g] = s_ref[...]
    rows_raw[g] = s_ref[part_of(g), :]

    def add_squares(h, i, first=False):
        def piece(j, carry):
            at = pl.ds(pl.multiple_of(i * half + j * part, part), part)
            values = raw[h, at, :].astype(F32)
            squares[at, :] = values * values if first else squares[at, :] + values * values
            return carry

        lax.fori_loop(0, half // part, piece, 0)

    for i in range(HALVES):
        add_squares(g, i, first=True)

    pl.semaphore_wait(barrier, n_grp - 1 + STEPS - 1)
    for k in range(1, STEPS):
        pl.semaphore_signal(below_in, inc=1, device_id=block(k), device_id_type=MESH)

    early = [
        send(s_ref.at[part_of(mate(d)), :], rows_raw.at[g], early_s.at[d], early_r.at[d], (b, mate(d)))
        for d in range(n_grp - 1)
    ]
    sent_slices = []

    def give(h, i, slot, to, src=None):
        n = len(sent_slices)
        src = raw.at[h] if src is None else src
        sent_slices.append(
            send(src.at[half_of(i), :], raw.at[h, half_of(i), :], gather_s.at[n], gather_r.at[slot, i], to)
        )

    def take(slot, h, i):
        here = raw.at[h, half_of(i), :]
        pltpu.make_async_copy(here, here, gather_r.at[slot, i]).wait()

    for i in range(HALVES):
        give(g, i, G_SIDE, beside, s_ref)
        give(g, i, G_LEFT, right, s_ref)
        give(g, i, G_RIGHT, left, s_ref)

    def urow(k):
        return urows.at[pl.ds(k * part, part), :]

    third_copies = [
        send(third.at[0, mate(d)], third.at[1, g], third_s.at[d], third_r.at[d], (b, mate(d)))
        for d in range(n_grp - 1)
    ]
    third[1, g] = third[0, g]

    for copy in early:
        copy.wait_recv()
    total = jnp.zeros((part, width), F32)
    for h in range(n_grp):
        values = rows_raw[h].astype(F32)
        total = total + values * values
    norms = jnp.sqrt(jnp.sum(total, axis=1, keepdims=True) + 1e-06)
    rows_norm[...] = norms
    for h in range(n_grp):
        urows[0:part, h * width : (h + 1) * width] = (rows_raw[h].astype(F32) / norms).astype(BF16)

    def pass_on(i):
        take(G_SIDE, at_x(0, True), i)
        give(at_x(0, True), i, G_LEFT_SIDE, right)
        give(at_x(0, True), i, G_RIGHT_SIDE, left)
        take(G_LEFT, at_x(-1), i)
        give(at_x(-1), i, G_LEFT_FAR, right)

    def pass_back(i):
        take(G_RIGHT_SIDE, at_x(1, True), i)
        give(at_x(1, True), i, G_RIGHT_FAR, left)

    def use(i, *slices):
        for h in slices:
            add_squares(h, i)

    pass_on(0)
    pass_on(1)
    def copy_to(src, dst, s, r, to):
        copy = pltpu.make_async_remote_copy(
            src_ref=src, dst_ref=dst, send_sem=s, recv_sem=r, device_id=to, device_id_type=MESH
        )
        started.append(copy)
        return copy

    def tile_copy(k):
        dst = tiles.at[pl.ds(k * part, part), :]
        return copy_to(sent_tiles.at[k - 1], dst, tile_s.at[k - 1], tile_r.at[k - 1], block(-k))

    unit_copies = [
        copy_to(urow(0), urow(1), unit_s.at[0], unit_r.at[0], block(-1)),
        copy_to(urow(0), urow(3), unit_s.at[2], unit_r.at[2], block(3)),
    ]
    unit_copies[1].start()
    tile_copies = [tile_copy(2), tile_copy(1)]
    wrap = lax.rem(b, n_loop // 2) < STEPS - 1

    def send_down():
        pl.semaphore_wait(below_in, STEPS - 1)
        unit_copies[0].start()
        for copy in tile_copies:
            copy.start()

    @pl.when(jnp.logical_not(wrap))
    def _():
        send_down()

    use(0, at_x(0, True), at_x(-1))
    pass_back(0)
    pass_back(1)
    @pl.when(wrap)
    def _():
        send_down()

    unit_copies[0].wait_recv()
    unit_copies.append(send(urow(1), urow(2), unit_s.at[1], unit_r.at[1], block(-1)))
    use(0, at_x(1, True))
    take(G_RIGHT, at_x(1), 0)
    take(G_LEFT_SIDE, at_x(-1, True), 0)
    use(0, at_x(1), at_x(-1, True))
    take(G_LEFT_FAR, at_x(-2), 0)
    use(0, at_x(-2))
    use(1, at_x(0, True), at_x(-1))
    for copy in third_copies:
        copy.wait_recv()
    for h in range(n_grp):
        tiles[3 * part : 4 * part, h * part : (h + 1) * part] = third[1, h].astype(F32).T.astype(BF16)
    take(G_RIGHT_FAR, at_x(2, True), 0)
    use(0, at_x(2, True))

    def normalise(i):
        def piece(j, carry):
            at = pl.ds(pl.multiple_of(i * half + j * part, part), part)
            norms = jnp.sqrt(jnp.sum(squares[at, :], axis=1, keepdims=True) + 1e-06)
            norm[at, :] = norms
            inverse = 1.0 / norms
            for h in range(n_grp):
                unit[at, h * width : (h + 1) * width] = (raw[h, at, :].astype(F32) * inverse).astype(BF16)
            return carry

        lax.fori_loop(0, half // part, piece, 0)

    def error_tiles(i):
        def piece(j, carry):
            at = pl.ds(pl.multiple_of(i * half + j * step, step), step)
            similar = lax.dot_general(
                urows[...], unit[at, :], (((1,), (1,)), ((), ())), preferred_element_type=F32
            )
            found = similar - tiles[:, at].astype(F32)
            errors[:, at] = found.astype(BF16)
            errors_t[at, :] = found.T.astype(BF16)
            return carry

        lax.fori_loop(0, half // step, piece, 0)

    def own_parts(i, c):
        at = features(c)
        found = jnp.dot(errors[:, half_of(i)], unit[half_of(i), at], preferred_element_type=F32)
        if i == 0:
            own_total[c] = found
        else:
            found = found + own_total[c]
            own_total[c, 0:part] = found[:part]
            for k in range(1, STEPS):
                own_send[k - 1, c] = found[k * part : (k + 1) * part].astype(BF16)

    def far_pair(dx, i):
        pair = lax.rem(x + dx + n_x, n_x)
        mine = urows[:, pl.ds(pl.multiple_of(pair * 2 * width, 2 * width), 2 * width)]

        at = half_of(i)
        sums = jnp.dot(errors_t[at, :], mine, preferred_element_type=F32).astype(BF16)
        far[pair * 2, at, :] = sums[:, :width]
        far[pair * 2 + 1, at, :] = sums[:, width:]

    sent_sums = []

    def hand(src, i, slot, to):
        n = len(sent_sums)
        sent_sums.append(
            send(src.at[half_of(i), :], landed.at[slot, half_of(i), :], far_s.at[n], far_r.at[slot, i], to)
        )

    def got(slot, i):
        here = landed.at[slot, half_of(i), :]
        pltpu.make_async_copy(here, here, far_r.at[slot, i]).wait()

    def far_passes(i):
        far_pair(2, i)
        hand(far.at[at_x(2, True)], i, R_LEFT_PASS, right)
        hand(far.at[at_x(2)], i, R_RIGHT_PASS, left)

    def far_near(i):
        far_pair(-1, i)
        hand(far.at[at_x(-1, True)], i, R_RIGHT, left)
        far_pair(1, i)

    def add_left_pass(i):
        at = half_of(i)
        got(R_LEFT_PASS, i)
        passed[0, at, :] = (far[at_x(1, True), at, :].astype(F32) + landed[R_LEFT_PASS, at, :].astype(F32)).astype(BF16)
        hand(passed.at[0], i, R_LEFT_SUM, right)

    def add_right_pass(i):
        at = half_of(i)
        got(R_RIGHT_PASS, i)
        passed[1, at, :] = (far[at_x(-1), at, :].astype(F32) + landed[R_RIGHT_PASS, at, :].astype(F32)).astype(BF16)
        hand(passed.at[1], i, R_RIGHT_SUM, left)

    def add_side(i):
        at = half_of(i)
        got(R_RIGHT, i)
        got(R_LEFT_SUM, i)
        side[at, :] = (
            far[at_x(0, True), at, :].astype(F32)
            + landed[R_RIGHT, at, :].astype(F32)
            + landed[R_LEFT_SUM, at, :].astype(F32)
        ).astype(BF16)
        hand(side, i, R_SIDE, beside)

    for copy in tile_copies + unit_copies[1:]:
        copy.wait_recv()
    normalise(0)
    error_tiles(0)
    far_passes(0)
    far_near(0)
    hand(far.at[at_x(1)], 0, R_LEFT, right)
    far_pair(0, 0)
    own_parts(0, 0)
    own_parts(0, 1)

    use(1, at_x(1, True))
    take(G_RIGHT, at_x(1), 1)
    take(G_LEFT_SIDE, at_x(-1, True), 1)
    use(1, at_x(1), at_x(-1, True))
    take(G_LEFT_FAR, at_x(-2), 1)
    take(G_RIGHT_FAR, at_x(2, True), 1)
    use(1, at_x(-2), at_x(2, True))
    normalise(1)
    error_tiles(1)
    own_copies = []
    for c in range(2):
        own_parts(1, c)
        own_copies.append(
            [
                send(
                    own_send.at[k - 1, c],
                    own_recv.at[k - 1, c],
                    own_s.at[k - 1, c],
                    own_r.at[k - 1, c],
                    block(k if k < 3 else -3),
                )
                for k in range(1, STEPS)
            ]
        )
    far_passes(1)
    add_left_pass(0)
    add_right_pass(0)
    far_near(1)
    add_left_pass(1)
    hand(far.at[at_x(1)], 1, R_LEFT, right)
    add_right_pass(1)
    far_pair(0, 1)

    eye = lax.broadcasted_iota(jnp.int32, (part, part), 0) == lax.broadcasted_iota(jnp.int32, (part, part), 1)

    def inner_rows(i, carry):
        at = pl.ds(pl.multiple_of(i * part, part), part)
        dots = jnp.zeros((part, width), F32)
        for h in range(n_grp):
            dots = dots + raw[h, at, :].astype(F32) * far[h, at, :].astype(F32)
        inner_send[pl.ds(i, 1), :] = to_lanes(jnp.sum(dots, axis=1, keepdims=True) / norm[at, :], eye)
        return carry

    lax.fori_loop(0, n_grp, inner_rows, 0)
    add_side(0)

    dots = jnp.zeros((part, width), F32)
    rows_copies = []
    near = n_grp // 2
    mine = lax.div(g, near)
    for c in range(2):
        for copy in own_copies[c]:
            copy.wait_recv()
        total = own_total[c, 0:part, :]
        for k in range(1, STEPS):
            total = total + own_recv[k - 1, c].astype(F32)
        group = 1 - mine if c == 0 else mine
        for i in range(near):
            h = group * near + i
            rounded = total[:, i * width : (i + 1) * width].astype(BF16)
            own_rows[h] = rounded
            dots = dots + rows_raw[h].astype(F32) * rounded.astype(F32)
        for i in range(near - c):
            h = group * near + (i if c == 0 else lax.rem(g + 1 + i, near))
            slot = lax.rem(g - h - 1 + 2 * n_grp, n_grp)
            rows_copies.append(
                send(own_rows.at[h], home_rows.at[part_of(g), :], rows_s.at[len(rows_copies)], rows_r.at[slot], (b, h))
            )
    inner_send[pl.ds(g, 1), :] = inner_send[pl.ds(g, 1), :] + to_lanes(
        jnp.sum(dots, axis=1, keepdims=True) / rows_norm[...], eye
    )
    inner_copies = [
        send(inner_send, inner_recv.at[d], inner_s.at[d], inner_r.at[d], (b, mate(d))) for d in range(n_grp - 1)
    ]
    home_rows[part_of(g), :] = own_rows[g]

    add_side(1)

    for copy in rows_copies + inner_copies:
        copy.wait_recv()
    inner = inner_send[...]
    for d in range(n_grp - 1):
        inner = inner + inner_recv[d]

    for i in range(n_grp):
        if i % (n_grp // HALVES) == 0:
            for slot in (R_LEFT, R_RIGHT_SUM, R_SIDE):
                got(slot, i // (n_grp // HALVES))
        at = pl.ds(i * part, part)
        grad = home_rows[at, :].astype(F32) + far[g, at, :].astype(F32)
        for slot in (R_LEFT, R_RIGHT_SUM, R_SIDE):
            grad = grad + landed[slot, at, :].astype(F32)
        inverse = 1.0 / norm[at, :]
        along = to_column(inner[i : i + 1, :], eye)
        out_ref[at, :] = (2.0 * inverse) * (grad - s_ref[at, :].astype(F32) * (inverse * along))

    for copy in started:
        copy.wait_send()


def per_device(n_loop, n_grp, student, teacher_tiles):
    rows, width = student.shape
    feats = width * n_grp
    part = rows // n_grp
    mates, hops = n_grp - 1, STEPS - 1
    dma = pltpu.SemaphoreType.DMA
    scratch = [
        pltpu.VMEM((n_grp, rows, width), BF16),
        pltpu.VMEM((rows, feats), BF16),
        pltpu.VMEM((rows, width), F32),
        pltpu.VMEM((rows, 1), F32),
        pltpu.VMEM((n_grp, part, width), BF16),
        pltpu.VMEM((part, 1), F32),
        pltpu.VMEM((STEPS * part, feats), BF16),
        pltpu.VMEM((hops - 1, part, rows), BF16),
        pltpu.VMEM((STEPS * part, rows), BF16),
        pltpu.VMEM((2, n_grp, part, part), BF16),
        pltpu.VMEM((STEPS * part, rows), BF16),
        pltpu.VMEM((rows, STEPS * part), BF16),
        pltpu.VMEM((hops, 2, part, feats // 2), BF16),
        pltpu.VMEM((hops, 2, part, feats // 2), BF16),
        pltpu.VMEM((n_grp, rows, width), BF16),
        pltpu.VMEM((7, rows, width), BF16),
        pltpu.VMEM((2, rows, width), BF16),
        pltpu.VMEM((rows, width), BF16),
        pltpu.VMEM((2, STEPS * part, feats // 2), F32),
        pltpu.VMEM((n_grp, part, width), BF16),
        pltpu.VMEM((rows, width), BF16),
        pltpu.VMEM((n_grp, part), F32),
        pltpu.VMEM((mates, n_grp, part), F32),
        pltpu.SemaphoreType.REGULAR,
        dma((mates,)), dma((mates,)),
        dma((7 * HALVES,)), dma((7, HALVES)),
        dma((hops - 1,)), dma((hops - 1,)),
        dma((mates,)), dma((mates,)),
        dma((hops,)), dma((hops,)),
        dma((hops, 2)), dma((hops, 2)),
        dma((7 * HALVES,)), dma((7, HALVES)),
        dma((mates,)), dma((mates,)),
        dma((mates,)), dma((mates,)),
    ]
    return pl.pallas_call(
        functools.partial(kernel, n_loop, n_grp),
        out_shape=jax.ShapeDtypeStruct((rows, width), F32),
        in_specs=[pl.BlockSpec(memory_space=pltpu.VMEM)] * 2,
        out_specs=pl.BlockSpec(memory_space=pltpu.VMEM),
        scratch_shapes=scratch,
        compiler_params=pltpu.CompilerParams(
            collective_id=0, has_side_effects=True, vmem_limit_bytes=56 * 2**20
        ),
        name="window_grad",
    )(student, teacher_tiles)


def solution(mesh):
    placed = (P("loop", "grp"), P(("loop", "grp"), None, None))
    return jax.shard_map(
        functools.partial(per_device, mesh.shape["loop"], mesh.shape["grp"]),
        mesh=mesh, in_specs=placed, out_specs=P("loop", "grp"), check_vma=False,
    )
```

```python
import functools

import jax
import jax.numpy as jnp
from jax import lax
from jax.experimental import pallas as pl
from jax.experimental.pallas import tpu as pltpu
from jax.sharding import PartitionSpec as P

MESH = pl.DeviceIdType.MESH
F32 = jnp.float32
BF16 = jnp.bfloat16
STEPS = 4
HALVES = 2
G_SIDE, G_LEFT, G_LEFT_SIDE, G_RIGHT, G_RIGHT_SIDE, G_LEFT_FAR, G_RIGHT_FAR = range(7)
R_LEFT_PASS, R_RIGHT_PASS, R_LEFT, R_RIGHT, R_LEFT_SUM, R_RIGHT_SUM, R_SIDE = range(7)


def to_lanes(column, eye):
    return jnp.sum(jnp.where(eye, column, 0.0), axis=0, keepdims=True)


def to_column(row, eye):
    return jnp.sum(jnp.where(eye, row, 0.0), axis=1, keepdims=True)


def kernel(
    n_loop, n_grp, s_hbm, t_hbm, out_hbm,
    s_ref, t_ref, out_ref, input_sem, output_sem,
    raw, unit, squares, norm, rows_raw, rows_norm, urows, sent_tiles, tiles, third, errors, errors_t, own_send, own_recv,
    far, landed, passed, side, own_total, own_rows, home_rows, inner_send, inner_recv,
    below_in, early_s, early_r, gather_s, gather_r, tile_s, tile_r, third_s, third_r, unit_s, unit_r, own_s, own_r, far_s, far_r,
    rows_s, rows_r, inner_s, inner_r,
):
    inputs = [
        pltpu.make_async_copy(s_hbm, s_ref, input_sem.at[0]),
        pltpu.make_async_copy(t_hbm, t_ref, input_sem.at[1]),
    ]
    for copy in inputs:
        copy.start()
    b = lax.axis_index("loop")
    g = lax.axis_index("grp")
    rows, width = s_ref.shape
    feats = width * n_grp
    part = rows // n_grp
    half = rows // HALVES
    step = half
    n_x = n_grp // 2
    x, y = lax.div(g, 2), lax.rem(g, 2)

    def at_x(dx, other=False):
        return lax.rem(x + dx + n_x, n_x) * 2 + (1 - y if other else y)

    def mate(d):
        return lax.rem(g + 1 + d, n_grp)

    def block(k):
        return (lax.rem(b + n_loop + k, n_loop), g)

    def part_of(h):
        return pl.ds(pl.multiple_of(h * part, part), part)

    def half_of(i):
        return pl.ds(i * half, half)

    def features(c):
        first = 1 - lax.div(g, n_grp // 2)
        return pl.ds(pl.multiple_of((first if c == 0 else 1 - first) * (feats // 2), feats // 2), feats // 2)

    started = []

    def send(src, dst, s, r, to):
        copy = pltpu.make_async_remote_copy(
            src_ref=src, dst_ref=dst, send_sem=s, recv_sem=r, device_id=to, device_id_type=MESH
        )
        copy.start()
        started.append(copy)
        return copy

    right, left, beside = (b, at_x(1)), (b, at_x(-1)), (b, at_x(0, True))

    barrier = pltpu.get_barrier_semaphore()
    for d in range(n_grp - 1):
        pl.semaphore_signal(barrier, inc=1, device_id=(b, mate(d)), device_id_type=MESH)
    for k in range(1, STEPS):
        pl.semaphore_signal(barrier, inc=1, device_id=block(-k), device_id_type=MESH)

    for copy in inputs:
        copy.wait()
    tiles[pl.ds(0, part), :] = t_ref[:, 0, :]
    for k in range(1, STEPS - 1):
        sent_tiles[k - 1] = t_ref[:, k, :]
    last = t_ref[:, STEPS - 1, :]
    for h in range(n_grp):
        third[0, h] = last[:, h * part : (h + 1) * part]
    raw[g] = s_ref[...]
    rows_raw[g] = s_ref[part_of(g), :]

    def add_squares(h, i, first=False):
        def piece(j, carry):
            at = pl.ds(pl.multiple_of(i * half + j * part, part), part)
            values = raw[h, at, :].astype(F32)
            squares[at, :] = values * values if first else squares[at, :] + values * values
            return carry

        lax.fori_loop(0, half // part, piece, 0)

    for i in range(HALVES):
        add_squares(g, i, first=True)

    pl.semaphore_wait(barrier, n_grp - 1 + STEPS - 1)
    for k in range(1, STEPS):
        pl.semaphore_signal(below_in, inc=1, device_id=block(k), device_id_type=MESH)

    early = [
        send(s_ref.at[part_of(mate(d)), :], rows_raw.at[g], early_s.at[d], early_r.at[d], (b, mate(d)))
        for d in range(n_grp - 1)
    ]
    sent_slices = []

    def give(h, i, slot, to, src=None):
        n = len(sent_slices)
        src = raw.at[h] if src is None else src
        sent_slices.append(
            send(src.at[half_of(i), :], raw.at[h, half_of(i), :], gather_s.at[n], gather_r.at[slot, i], to)
        )

    def take(slot, h, i):
        here = raw.at[h, half_of(i), :]
        pltpu.make_async_copy(here, here, gather_r.at[slot, i]).wait()

    for i in range(HALVES):
        give(g, i, G_SIDE, beside, s_ref)
        give(g, i, G_LEFT, right, s_ref)
        give(g, i, G_RIGHT, left, s_ref)

    def urow(k):
        return urows.at[pl.ds(k * part, part), :]

    third_copies = [
        send(third.at[0, mate(d)], third.at[1, g], third_s.at[d], third_r.at[d], (b, mate(d)))
        for d in range(n_grp - 1)
    ]
    def copy_to(src, dst, s, r, to):
        copy = pltpu.make_async_remote_copy(
            src_ref=src, dst_ref=dst, send_sem=s, recv_sem=r, device_id=to, device_id_type=MESH
        )
        started.append(copy)
        return copy

    def tile_copy(k):
        dst = tiles.at[pl.ds(k * part, part), :]
        return copy_to(sent_tiles.at[k - 1], dst, tile_s.at[k - 1], tile_r.at[k - 1], block(-k))

    tile_copies = [tile_copy(2), tile_copy(1)]
    wrap = lax.rem(b, n_loop // 2) < STEPS - 1

    @pl.when(jnp.logical_not(wrap))
    def _():
        pl.semaphore_wait(below_in, STEPS - 1)
        for copy in tile_copies:
            copy.start()

    third[1, g] = third[0, g]

    for copy in early:
        copy.wait_recv()
    total = jnp.zeros((part, width), F32)
    for h in range(n_grp):
        values = rows_raw[h].astype(F32)
        total = total + values * values
    norms = jnp.sqrt(jnp.sum(total, axis=1, keepdims=True) + 1e-06)
    rows_norm[...] = norms
    for h in range(n_grp):
        urows[0:part, h * width : (h + 1) * width] = (rows_raw[h].astype(F32) / norms).astype(BF16)

    unit_copies = [
        copy_to(urow(0), urow(1), unit_s.at[0], unit_r.at[0], block(-1)),
        copy_to(urow(0), urow(3), unit_s.at[2], unit_r.at[2], block(3)),
    ]
    unit_copies[1].start()

    @pl.when(jnp.logical_not(wrap))
    def _():
        unit_copies[0].start()

    def pass_on(i):
        take(G_SIDE, at_x(0, True), i)
        give(at_x(0, True), i, G_LEFT_SIDE, right)
        give(at_x(0, True), i, G_RIGHT_SIDE, left)
        take(G_LEFT, at_x(-1), i)
        give(at_x(-1), i, G_LEFT_FAR, right)

    def pass_back(i):
        take(G_RIGHT_SIDE, at_x(1, True), i)
        give(at_x(1, True), i, G_RIGHT_FAR, left)

    def use(i, *slices):
        for h in slices:
            add_squares(h, i)

    pass_on(0)
    pass_on(1)
    unit_copies.append(copy_to(urow(1), urow(2), unit_s.at[1], unit_r.at[1], block(-1)))

    def relay():
        unit_copies[0].wait_recv()
        unit_copies[2].start()

    @pl.when(jnp.logical_not(wrap))
    def _():
        relay()

    use(0, at_x(0, True), at_x(-1))
    pass_back(0)
    pass_back(1)
    @pl.when(wrap)
    def _():
        pl.semaphore_wait(below_in, STEPS - 1)
        unit_copies[0].start()
        for copy in tile_copies:
            copy.start()

    @pl.when(wrap)
    def _():
        relay()

    use(0, at_x(1, True))
    take(G_RIGHT, at_x(1), 0)
    take(G_LEFT_SIDE, at_x(-1, True), 0)
    use(0, at_x(1), at_x(-1, True))
    take(G_LEFT_FAR, at_x(-2), 0)
    use(0, at_x(-2))
    use(1, at_x(0, True), at_x(-1))
    for copy in third_copies:
        copy.wait_recv()
    for h in range(n_grp):
        tiles[3 * part : 4 * part, h * part : (h + 1) * part] = third[1, h].astype(F32).T.astype(BF16)
    take(G_RIGHT_FAR, at_x(2, True), 0)
    use(0, at_x(2, True))

    def normalise(i):
        def piece(j, carry):
            at = pl.ds(pl.multiple_of(i * half + j * part, part), part)
            norms = jnp.sqrt(jnp.sum(squares[at, :], axis=1, keepdims=True) + 1e-06)
            norm[at, :] = norms
            inverse = 1.0 / norms
            for h in range(n_grp):
                unit[at, h * width : (h + 1) * width] = (raw[h, at, :].astype(F32) * inverse).astype(BF16)
            return carry

        lax.fori_loop(0, half // part, piece, 0)

    def error_tiles(i):
        def piece(j, carry):
            at = pl.ds(pl.multiple_of(i * half + j * step, step), step)
            similar = lax.dot_general(
                urows[...], unit[at, :], (((1,), (1,)), ((), ())), preferred_element_type=F32
            )
            found = similar - tiles[:, at].astype(F32)
            errors[:, at] = found.astype(BF16)
            errors_t[at, :] = found.T.astype(BF16)
            return carry

        lax.fori_loop(0, half // step, piece, 0)

    def own_parts(i, c):
        at = features(c)
        found = jnp.dot(errors[:, half_of(i)], unit[half_of(i), at], preferred_element_type=F32)
        if i == 0:
            own_total[c] = found
        else:
            found = found + own_total[c]
            own_total[c, 0:part] = found[:part]
            for k in range(1, STEPS):
                own_send[k - 1, c] = found[k * part : (k + 1) * part].astype(BF16)

    def far_pair(dx, i):
        pair = lax.rem(x + dx + n_x, n_x)
        mine = urows[:, pl.ds(pl.multiple_of(pair * 2 * width, 2 * width), 2 * width)]

        at = half_of(i)
        sums = jnp.dot(errors_t[at, :], mine, preferred_element_type=F32).astype(BF16)
        far[pair * 2, at, :] = sums[:, :width]
        far[pair * 2 + 1, at, :] = sums[:, width:]

    sent_sums = []

    def hand(src, i, slot, to):
        n = len(sent_sums)
        sent_sums.append(
            send(src.at[half_of(i), :], landed.at[slot, half_of(i), :], far_s.at[n], far_r.at[slot, i], to)
        )

    def got(slot, i):
        here = landed.at[slot, half_of(i), :]
        pltpu.make_async_copy(here, here, far_r.at[slot, i]).wait()

    def far_passes(i):
        far_pair(2, i)
        hand(far.at[at_x(2, True)], i, R_LEFT_PASS, right)
        hand(far.at[at_x(2)], i, R_RIGHT_PASS, left)

    def far_near(i):
        far_pair(-1, i)
        hand(far.at[at_x(-1, True)], i, R_RIGHT, left)
        far_pair(1, i)

    def add_left_pass(i):
        at = half_of(i)
        got(R_LEFT_PASS, i)
        passed[0, at, :] = (far[at_x(1, True), at, :].astype(F32) + landed[R_LEFT_PASS, at, :].astype(F32)).astype(BF16)
        hand(passed.at[0], i, R_LEFT_SUM, right)

    def add_right_pass(i):
        at = half_of(i)
        got(R_RIGHT_PASS, i)
        passed[1, at, :] = (far[at_x(-1), at, :].astype(F32) + landed[R_RIGHT_PASS, at, :].astype(F32)).astype(BF16)
        hand(passed.at[1], i, R_RIGHT_SUM, left)

    def add_side(i):
        at = half_of(i)
        got(R_RIGHT, i)
        got(R_LEFT_SUM, i)
        side[at, :] = (
            far[at_x(0, True), at, :].astype(F32)
            + landed[R_RIGHT, at, :].astype(F32)
            + landed[R_LEFT_SUM, at, :].astype(F32)
        ).astype(BF16)
        hand(side, i, R_SIDE, beside)

    for copy in tile_copies + unit_copies[1:]:
        copy.wait_recv()
    normalise(0)
    error_tiles(0)
    far_passes(0)
    far_near(0)
    hand(far.at[at_x(1)], 0, R_LEFT, right)
    far_pair(0, 0)
    own_parts(0, 0)
    own_parts(0, 1)

    use(1, at_x(1, True))
    take(G_RIGHT, at_x(1), 1)
    take(G_LEFT_SIDE, at_x(-1, True), 1)
    use(1, at_x(1), at_x(-1, True))
    take(G_LEFT_FAR, at_x(-2), 1)
    take(G_RIGHT_FAR, at_x(2, True), 1)
    use(1, at_x(-2), at_x(2, True))
    normalise(1)
    error_tiles(1)
    own_copies = []
    for c in range(2):
        own_parts(1, c)
        own_copies.append(
            [
                send(
                    own_send.at[k - 1, c],
                    own_recv.at[k - 1, c],
                    own_s.at[k - 1, c],
                    own_r.at[k - 1, c],
                    block(k if k < 3 else -3),
                )
                for k in range(1, STEPS)
            ]
        )
    far_passes(1)
    add_left_pass(0)
    add_right_pass(0)
    far_near(1)
    add_left_pass(1)
    hand(far.at[at_x(1)], 1, R_LEFT, right)
    add_right_pass(1)
    far_pair(0, 1)

    eye = lax.broadcasted_iota(jnp.int32, (part, part), 0) == lax.broadcasted_iota(jnp.int32, (part, part), 1)

    def inner_rows(i, carry):
        at = pl.ds(pl.multiple_of(i * part, part), part)
        dots = jnp.zeros((part, width), F32)
        for h in range(n_grp):
            dots = dots + raw[h, at, :].astype(F32) * far[h, at, :].astype(F32)
        inner_send[pl.ds(i, 1), :] = to_lanes(jnp.sum(dots, axis=1, keepdims=True) / norm[at, :], eye)
        return carry

    lax.fori_loop(0, n_grp, inner_rows, 0)
    add_side(0)

    dots = jnp.zeros((part, width), F32)
    rows_copies = []
    near = n_grp // 2
    mine = lax.div(g, near)
    for c in range(2):
        for copy in own_copies[c]:
            copy.wait_recv()
        total = own_total[c, 0:part, :]
        for k in range(1, STEPS):
            total = total + own_recv[k - 1, c].astype(F32)
        group = 1 - mine if c == 0 else mine
        for i in range(near):
            h = group * near + i
            rounded = total[:, i * width : (i + 1) * width].astype(BF16)
            own_rows[h] = rounded
            dots = dots + rows_raw[h].astype(F32) * rounded.astype(F32)
        for i in range(near - c):
            h = group * near + (i if c == 0 else lax.rem(g + 1 + i, near))
            slot = lax.rem(g - h - 1 + 2 * n_grp, n_grp)
            rows_copies.append(
                send(own_rows.at[h], home_rows.at[part_of(g), :], rows_s.at[len(rows_copies)], rows_r.at[slot], (b, h))
            )
    inner_send[pl.ds(g, 1), :] = inner_send[pl.ds(g, 1), :] + to_lanes(
        jnp.sum(dots, axis=1, keepdims=True) / rows_norm[...], eye
    )
    inner_copies = [
        send(inner_send, inner_recv.at[d], inner_s.at[d], inner_r.at[d], (b, mate(d))) for d in range(n_grp - 1)
    ]
    home_rows[part_of(g), :] = own_rows[g]

    add_side(1)

    def add_home(i):
        for slot in (R_LEFT, R_RIGHT_SUM, R_SIDE):
            got(slot, i)
        at = half_of(i)
        grad = far[g, at, :].astype(F32)
        for slot in (R_LEFT, R_RIGHT_SUM, R_SIDE):
            grad = grad + landed[slot, at, :].astype(F32)
        out_ref[at, :] = grad

    add_home(0)
    for copy in rows_copies + inner_copies:
        copy.wait_recv()
    inner = inner_send[...]
    for d in range(n_grp - 1):
        inner = inner + inner_recv[d]

    outputs = []
    for i in range(HALVES):
        if i > 0:
            add_home(i)
        for j in range(i * n_grp // HALVES, (i + 1) * n_grp // HALVES):
            at = pl.ds(j * part, part)
            grad = home_rows[at, :].astype(F32) + out_ref[at, :]
            inverse = 1.0 / norm[at, :]
            along = to_column(inner[j : j + 1, :], eye)
            out_ref[at, :] = (2.0 * inverse) * (grad - s_ref[at, :].astype(F32) * (inverse * along))
        outputs.append(
            pltpu.make_async_copy(out_ref.at[half_of(i), :], out_hbm.at[half_of(i), :], output_sem.at[i])
        )
        outputs[i].start()

    for copy in started:
        copy.wait_send()
    for copy in outputs:
        copy.wait()


def per_device(n_loop, n_grp, student, teacher_tiles):
    rows, width = student.shape
    feats = width * n_grp
    part = rows // n_grp
    mates, hops = n_grp - 1, STEPS - 1
    dma = pltpu.SemaphoreType.DMA
    scratch = [
        pltpu.VMEM((rows, width), BF16),
        pltpu.VMEM((part, STEPS, rows), BF16),
        pltpu.VMEM((rows, width), F32),
        dma((2,)),
        dma((HALVES,)),
        pltpu.VMEM((n_grp, rows, width), BF16),
        pltpu.VMEM((rows, feats), BF16),
        pltpu.VMEM((rows, width), F32),
        pltpu.VMEM((rows, 1), F32),
        pltpu.VMEM((n_grp, part, width), BF16),
        pltpu.VMEM((part, 1), F32),
        pltpu.VMEM((STEPS * part, feats), BF16),
        pltpu.VMEM((hops - 1, part, rows), BF16),
        pltpu.VMEM((STEPS * part, rows), BF16),
        pltpu.VMEM((2, n_grp, part, part), BF16),
        pltpu.VMEM((STEPS * part, rows), BF16),
        pltpu.VMEM((rows, STEPS * part), BF16),
        pltpu.VMEM((hops, 2, part, feats // 2), BF16),
        pltpu.VMEM((hops, 2, part, feats // 2), BF16),
        pltpu.VMEM((n_grp, rows, width), BF16),
        pltpu.VMEM((7, rows, width), BF16),
        pltpu.VMEM((2, rows, width), BF16),
        pltpu.VMEM((rows, width), BF16),
        pltpu.VMEM((2, STEPS * part, feats // 2), F32),
        pltpu.VMEM((n_grp, part, width), BF16),
        pltpu.VMEM((rows, width), BF16),
        pltpu.VMEM((n_grp, part), F32),
        pltpu.VMEM((mates, n_grp, part), F32),
        pltpu.SemaphoreType.REGULAR,
        dma((mates,)), dma((mates,)),
        dma((7 * HALVES,)), dma((7, HALVES)),
        dma((hops - 1,)), dma((hops - 1,)),
        dma((mates,)), dma((mates,)),
        dma((hops,)), dma((hops,)),
        dma((hops, 2)), dma((hops, 2)),
        dma((7 * HALVES,)), dma((7, HALVES)),
        dma((mates,)), dma((mates,)),
        dma((mates,)), dma((mates,)),
    ]
    return pl.pallas_call(
        functools.partial(kernel, n_loop, n_grp),
        out_shape=jax.ShapeDtypeStruct((rows, width), F32),
        in_specs=[pl.BlockSpec(memory_space=pl.ANY)] * 2,
        out_specs=pl.BlockSpec(memory_space=pl.ANY),
        scratch_shapes=scratch,
        compiler_params=pltpu.CompilerParams(
            collective_id=0, has_side_effects=True, vmem_limit_bytes=56 * 2**20
        ),
        name="window_grad",
    )(student, teacher_tiles)


def solution(mesh):
    placed = (P("loop", "grp"), P(("loop", "grp"), None, None))
    return jax.shard_map(
        functools.partial(per_device, mesh.shape["loop"], mesh.shape["grp"]),
        mesh=mesh, in_specs=placed, out_specs=P("loop", "grp"), check_vma=False,
    )
```

```python
import functools

import jax
import jax.numpy as jnp
from jax import lax
from jax.experimental import pallas as pl
from jax.experimental.pallas import tpu as pltpu
from jax.sharding import PartitionSpec as P

MESH = pl.DeviceIdType.MESH
F32 = jnp.float32
BF16 = jnp.bfloat16
STEPS = 4
HALVES = 2
G_SIDE, G_LEFT, G_LEFT_SIDE, G_RIGHT, G_RIGHT_SIDE, G_LEFT_FAR, G_RIGHT_FAR = range(7)
R_LEFT_PASS, R_RIGHT_PASS, R_LEFT, R_RIGHT, R_LEFT_SUM, R_RIGHT_SUM, R_SIDE = range(7)


def to_lanes(column, eye):
    return jnp.sum(jnp.where(eye, column, 0.0), axis=0, keepdims=True)


def to_column(row, eye):
    return jnp.sum(jnp.where(eye, row, 0.0), axis=1, keepdims=True)


def kernel(
    n_loop, n_grp, s_hbm, t_hbm, out_hbm,
    s_ref, t_ref, out_ref, input_sem, output_sem,
    raw, unit, squares, norm, rows_raw, rows_norm, urows, sent_tiles, tiles, third, errors, errors_t, own_send, own_recv,
    far, landed, passed, side, own_total, own_rows, home_rows, inner_send, inner_recv,
    below_in, early_s, early_r, gather_s, gather_r, tile_s, tile_r, third_s, third_r, unit_s, unit_r, own_s, own_r, far_s, far_r,
    rows_s, rows_r, inner_s, inner_r,
):
    inputs = [
        pltpu.make_async_copy(s_hbm, s_ref, input_sem.at[0]),
        pltpu.make_async_copy(t_hbm, t_ref, input_sem.at[1]),
    ]
    for copy in inputs:
        copy.start()
    b = lax.axis_index("loop")
    g = lax.axis_index("grp")
    rows, width = s_ref.shape
    feats = width * n_grp
    part = rows // n_grp
    half = rows // HALVES
    step = half
    n_x = n_grp // 2
    x, y = lax.div(g, 2), lax.rem(g, 2)

    def at_x(dx, other=False):
        return lax.rem(x + dx + n_x, n_x) * 2 + (1 - y if other else y)

    def mate(d):
        return lax.rem(g + 1 + d, n_grp)

    def block(k):
        return (lax.rem(b + n_loop + k, n_loop), g)

    def part_of(h):
        return pl.ds(pl.multiple_of(h * part, part), part)

    def half_of(i):
        return pl.ds(i * half, half)

    def features(c):
        first = 1 - lax.div(g, n_grp // 2)
        return pl.ds(pl.multiple_of((first if c == 0 else 1 - first) * (feats // 2), feats // 2), feats // 2)

    started = []

    def send(src, dst, s, r, to):
        copy = pltpu.make_async_remote_copy(
            src_ref=src, dst_ref=dst, send_sem=s, recv_sem=r, device_id=to, device_id_type=MESH
        )
        copy.start()
        started.append(copy)
        return copy

    right, left, beside = (b, at_x(1)), (b, at_x(-1)), (b, at_x(0, True))

    barrier = pltpu.get_barrier_semaphore()
    for d in range(n_grp - 1):
        pl.semaphore_signal(barrier, inc=1, device_id=(b, mate(d)), device_id_type=MESH)
    for k in range(1, STEPS):
        pl.semaphore_signal(barrier, inc=1, device_id=block(-k), device_id_type=MESH)

    for copy in inputs:
        copy.wait()
    tiles[pl.ds(0, part), :] = t_ref[:, 0, :]
    for k in range(1, STEPS - 1):
        sent_tiles[k - 1] = t_ref[:, k, :]
    last = t_ref[:, STEPS - 1, :]
    for h in range(n_grp):
        third[0, h] = last[:, h * part : (h + 1) * part]
    raw[g] = s_ref[...]
    rows_raw[g] = s_ref[part_of(g), :]

    def add_squares(h, i, first=False):
        def piece(j, carry):
            at = pl.ds(pl.multiple_of(i * half + j * part, part), part)
            values = raw[h, at, :].astype(F32)
            squares[at, :] = values * values if first else squares[at, :] + values * values
            return carry

        lax.fori_loop(0, half // part, piece, 0)

    for i in range(HALVES):
        add_squares(g, i, first=True)

    pl.semaphore_wait(barrier, n_grp - 1 + STEPS - 1)
    for k in range(1, STEPS):
        pl.semaphore_signal(below_in, inc=1, device_id=block(k), device_id_type=MESH)

    early = [
        send(s_ref.at[part_of(mate(d)), :], rows_raw.at[g], early_s.at[d], early_r.at[d], (b, mate(d)))
        for d in range(n_grp - 1)
    ]
    sent_slices = []

    def give(h, i, slot, to, src=None):
        n = len(sent_slices)
        src = raw.at[h] if src is None else src
        sent_slices.append(
            send(src.at[half_of(i), :], raw.at[h, half_of(i), :], gather_s.at[n], gather_r.at[slot, i], to)
        )

    def take(slot, h, i):
        here = raw.at[h, half_of(i), :]
        pltpu.make_async_copy(here, here, gather_r.at[slot, i]).wait()

    for i in range(HALVES):
        give(g, i, G_SIDE, beside, s_ref)
        give(g, i, G_LEFT, right, s_ref)
        give(g, i, G_RIGHT, left, s_ref)

    def urow(k):
        return urows.at[pl.ds(k * part, part), :]

    third_copies = [
        send(third.at[0, mate(d)], third.at[1, g], third_s.at[d], third_r.at[d], (b, mate(d)))
        for d in range(n_grp - 1)
    ]
    def copy_to(src, dst, s, r, to):
        copy = pltpu.make_async_remote_copy(
            src_ref=src, dst_ref=dst, send_sem=s, recv_sem=r, device_id=to, device_id_type=MESH
        )
        started.append(copy)
        return copy

    def tile_copy(k):
        dst = tiles.at[pl.ds(k * part, part), :]
        return copy_to(sent_tiles.at[k - 1], dst, tile_s.at[k - 1], tile_r.at[k - 1], block(-k))

    tile_copies = [tile_copy(2), tile_copy(1)]
    wrap = lax.rem(b, n_loop // 2) < STEPS - 1

    @pl.when(jnp.logical_not(wrap))
    def _():
        pl.semaphore_wait(below_in, STEPS - 1)
        for copy in tile_copies:
            copy.start()

    third[1, g] = third[0, g]

    for copy in early:
        copy.wait_recv()
    total = jnp.zeros((part, width), F32)
    for h in range(n_grp):
        values = rows_raw[h].astype(F32)
        total = total + values * values
    norms = jnp.sqrt(jnp.sum(total, axis=1, keepdims=True) + 1e-06)
    rows_norm[...] = norms
    for h in range(n_grp):
        urows[0:part, h * width : (h + 1) * width] = (rows_raw[h].astype(F32) / norms).astype(BF16)

    unit_copies = [
        copy_to(urow(0), urow(1), unit_s.at[0], unit_r.at[0], block(-1)),
        copy_to(urow(0), urow(3), unit_s.at[2], unit_r.at[2], block(3)),
    ]
    unit_copies[1].start()

    @pl.when(jnp.logical_not(wrap))
    def _():
        unit_copies[0].start()

    def pass_on(i):
        take(G_SIDE, at_x(0, True), i)
        give(at_x(0, True), i, G_LEFT_SIDE, right)
        give(at_x(0, True), i, G_RIGHT_SIDE, left)
        take(G_LEFT, at_x(-1), i)
        give(at_x(-1), i, G_LEFT_FAR, right)

    def pass_back(i):
        take(G_RIGHT_SIDE, at_x(1, True), i)
        give(at_x(1, True), i, G_RIGHT_FAR, left)

    def use(i, *slices):
        for h in slices:
            add_squares(h, i)

    pass_on(0)
    pass_on(1)
    unit_copies.append(copy_to(urow(1), urow(2), unit_s.at[1], unit_r.at[1], block(-1)))

    def relay():
        unit_copies[0].wait_recv()
        unit_copies[2].start()

    @pl.when(jnp.logical_not(wrap))
    def _():
        relay()

    use(0, at_x(0, True), at_x(-1))
    pass_back(0)
    pass_back(1)
    @pl.when(wrap)
    def _():
        pl.semaphore_wait(below_in, STEPS - 1)
        unit_copies[0].start()
        for copy in tile_copies:
            copy.start()

    @pl.when(wrap)
    def _():
        relay()

    use(0, at_x(1, True))
    take(G_RIGHT, at_x(1), 0)
    take(G_LEFT_SIDE, at_x(-1, True), 0)
    use(0, at_x(1), at_x(-1, True))
    take(G_LEFT_FAR, at_x(-2), 0)
    use(0, at_x(-2))
    use(1, at_x(0, True), at_x(-1))
    for copy in third_copies:
        copy.wait_recv()
    for h in range(n_grp):
        tiles[3 * part : 4 * part, h * part : (h + 1) * part] = third[1, h].astype(F32).T.astype(BF16)
    take(G_RIGHT_FAR, at_x(2, True), 0)
    use(0, at_x(2, True))

    def normalise(i):
        def piece(j, carry):
            at = pl.ds(pl.multiple_of(i * half + j * part, part), part)
            norms = jnp.sqrt(jnp.sum(squares[at, :], axis=1, keepdims=True) + 1e-06)
            norm[at, :] = norms
            inverse = 1.0 / norms
            for h in range(n_grp):
                unit[at, h * width : (h + 1) * width] = (raw[h, at, :].astype(F32) * inverse).astype(BF16)
            return carry

        lax.fori_loop(0, half // part, piece, 0)

    def error_tiles(i):
        def piece(j, carry):
            at = pl.ds(pl.multiple_of(i * half + j * step, step), step)
            similar = lax.dot_general(
                urows[...], unit[at, :], (((1,), (1,)), ((), ())), preferred_element_type=F32
            )
            found = similar - tiles[:, at].astype(F32)
            errors[:, at] = found.astype(BF16)
            errors_t[at, :] = found.T.astype(BF16)
            return carry

        lax.fori_loop(0, half // step, piece, 0)

    def own_parts(c):
        found = jnp.dot(errors[...], unit[:, features(c)], preferred_element_type=F32)
        own_total[c] = found[:part]
        for k in range(1, STEPS):
            own_send[k - 1, c] = found[k * part : (k + 1) * part].astype(BF16)

    def far_pair(dx, i):
        pair = lax.rem(x + dx + n_x, n_x)
        mine = urows[:, pl.ds(pl.multiple_of(pair * 2 * width, 2 * width), 2 * width)]

        at = half_of(i)
        sums = jnp.dot(errors_t[at, :], mine, preferred_element_type=F32).astype(BF16)
        far[pair * 2, at, :] = sums[:, :width]
        far[pair * 2 + 1, at, :] = sums[:, width:]

    sent_sums = []

    def hand(src, i, slot, to):
        n = len(sent_sums)
        sent_sums.append(
            send(src.at[half_of(i), :], landed.at[slot, half_of(i), :], far_s.at[n], far_r.at[slot, i], to)
        )

    def got(slot, i):
        here = landed.at[slot, half_of(i), :]
        pltpu.make_async_copy(here, here, far_r.at[slot, i]).wait()

    def far_passes(i):
        far_pair(2, i)
        hand(far.at[at_x(2, True)], i, R_LEFT_PASS, right)
        hand(far.at[at_x(2)], i, R_RIGHT_PASS, left)

    def far_near(i):
        far_pair(-1, i)
        hand(far.at[at_x(-1, True)], i, R_RIGHT, left)
        far_pair(1, i)

    def add_left_pass(i):
        at = half_of(i)
        got(R_LEFT_PASS, i)
        passed[0, at, :] = (far[at_x(1, True), at, :].astype(F32) + landed[R_LEFT_PASS, at, :].astype(F32)).astype(BF16)
        hand(passed.at[0], i, R_LEFT_SUM, right)

    def add_right_pass(i):
        at = half_of(i)
        got(R_RIGHT_PASS, i)
        passed[1, at, :] = (far[at_x(-1), at, :].astype(F32) + landed[R_RIGHT_PASS, at, :].astype(F32)).astype(BF16)
        hand(passed.at[1], i, R_RIGHT_SUM, left)

    def add_side(i):
        at = half_of(i)
        got(R_RIGHT, i)
        got(R_LEFT_SUM, i)
        side[at, :] = (
            far[at_x(0, True), at, :].astype(F32)
            + landed[R_RIGHT, at, :].astype(F32)
            + landed[R_LEFT_SUM, at, :].astype(F32)
        ).astype(BF16)
        hand(side, i, R_SIDE, beside)

    for copy in tile_copies + unit_copies[1:]:
        copy.wait_recv()
    normalise(0)
    error_tiles(0)
    far_passes(0)
    far_near(0)
    hand(far.at[at_x(1)], 0, R_LEFT, right)

    use(1, at_x(1, True))
    take(G_RIGHT, at_x(1), 1)
    take(G_LEFT_SIDE, at_x(-1, True), 1)
    use(1, at_x(1), at_x(-1, True))
    take(G_LEFT_FAR, at_x(-2), 1)
    take(G_RIGHT_FAR, at_x(2, True), 1)
    use(1, at_x(-2), at_x(2, True))
    normalise(1)
    error_tiles(1)
    own_copies = []
    for c in range(2):
        own_parts(c)
        own_copies.append(
            [
                send(
                    own_send.at[k - 1, c],
                    own_recv.at[k - 1, c],
                    own_s.at[k - 1, c],
                    own_r.at[k - 1, c],
                    block(k if k < 3 else -3),
                )
                for k in range(1, STEPS)
            ]
        )
    far_passes(1)
    add_left_pass(0)
    add_right_pass(0)
    far_near(1)
    add_left_pass(1)
    hand(far.at[at_x(1)], 1, R_LEFT, right)
    add_right_pass(1)
    far_pair(0, 0)
    far_pair(0, 1)

    eye = lax.broadcasted_iota(jnp.int32, (part, part), 0) == lax.broadcasted_iota(jnp.int32, (part, part), 1)

    def inner_rows(i, carry):
        at = pl.ds(pl.multiple_of(i * part, part), part)
        dots = jnp.zeros((part, width), F32)
        for h in range(n_grp):
            dots = dots + raw[h, at, :].astype(F32) * far[h, at, :].astype(F32)
        inner_send[pl.ds(i, 1), :] = to_lanes(jnp.sum(dots, axis=1, keepdims=True) / norm[at, :], eye)
        return carry

    lax.fori_loop(0, n_grp, inner_rows, 0)
    add_side(0)

    dots = jnp.zeros((part, width), F32)
    rows_copies = []
    near = n_grp // 2
    mine = lax.div(g, near)
    for c in range(2):
        for copy in own_copies[c]:
            copy.wait_recv()
        total = own_total[c]
        for k in range(1, STEPS):
            total = total + own_recv[k - 1, c].astype(F32)
        group = 1 - mine if c == 0 else mine
        for i in range(near):
            h = group * near + i
            rounded = total[:, i * width : (i + 1) * width].astype(BF16)
            own_rows[h] = rounded
            dots = dots + rows_raw[h].astype(F32) * rounded.astype(F32)
        for i in range(near - c):
            h = group * near + (i if c == 0 else lax.rem(g + 1 + i, near))
            slot = lax.rem(g - h - 1 + 2 * n_grp, n_grp)
            rows_copies.append(
                send(own_rows.at[h], home_rows.at[part_of(g), :], rows_s.at[len(rows_copies)], rows_r.at[slot], (b, h))
            )
    inner_send[pl.ds(g, 1), :] = inner_send[pl.ds(g, 1), :] + to_lanes(
        jnp.sum(dots, axis=1, keepdims=True) / rows_norm[...], eye
    )
    inner_copies = [
        send(inner_send, inner_recv.at[d], inner_s.at[d], inner_r.at[d], (b, mate(d))) for d in range(n_grp - 1)
    ]
    home_rows[part_of(g), :] = own_rows[g]

    add_side(1)

    def add_home(i):
        for slot in (R_LEFT, R_RIGHT_SUM, R_SIDE):
            got(slot, i)
        at = half_of(i)
        grad = far[g, at, :].astype(F32)
        for slot in (R_LEFT, R_RIGHT_SUM, R_SIDE):
            grad = grad + landed[slot, at, :].astype(F32)
        out_ref[at, :] = grad

    add_home(0)
    for copy in rows_copies + inner_copies:
        copy.wait_recv()
    inner = inner_send[...]
    for d in range(n_grp - 1):
        inner = inner + inner_recv[d]

    outputs = []
    for i in range(HALVES):
        if i > 0:
            add_home(i)
        for j in range(i * n_grp // HALVES, (i + 1) * n_grp // HALVES):
            at = pl.ds(j * part, part)
            grad = home_rows[at, :].astype(F32) + out_ref[at, :]
            inverse = 1.0 / norm[at, :]
            along = to_column(inner[j : j + 1, :], eye)
            out_ref[at, :] = (2.0 * inverse) * (grad - s_ref[at, :].astype(F32) * (inverse * along))
        outputs.append(
            pltpu.make_async_copy(out_ref.at[half_of(i), :], out_hbm.at[half_of(i), :], output_sem.at[i])
        )
        outputs[i].start()

    for copy in started:
        copy.wait_send()
    for copy in outputs:
        copy.wait()


def per_device(n_loop, n_grp, student, teacher_tiles):
    rows, width = student.shape
    feats = width * n_grp
    part = rows // n_grp
    mates, hops = n_grp - 1, STEPS - 1
    dma = pltpu.SemaphoreType.DMA
    scratch = [
        pltpu.VMEM((rows, width), BF16),
        pltpu.VMEM((part, STEPS, rows), BF16),
        pltpu.VMEM((rows, width), F32),
        dma((2,)),
        dma((HALVES,)),
        pltpu.VMEM((n_grp, rows, width), BF16),
        pltpu.VMEM((rows, feats), BF16),
        pltpu.VMEM((rows, width), F32),
        pltpu.VMEM((rows, 1), F32),
        pltpu.VMEM((n_grp, part, width), BF16),
        pltpu.VMEM((part, 1), F32),
        pltpu.VMEM((STEPS * part, feats), BF16),
        pltpu.VMEM((hops - 1, part, rows), BF16),
        pltpu.VMEM((STEPS * part, rows), BF16),
        pltpu.VMEM((2, n_grp, part, part), BF16),
        pltpu.VMEM((STEPS * part, rows), BF16),
        pltpu.VMEM((rows, STEPS * part), BF16),
        pltpu.VMEM((hops, 2, part, feats // 2), BF16),
        pltpu.VMEM((hops, 2, part, feats // 2), BF16),
        pltpu.VMEM((n_grp, rows, width), BF16),
        pltpu.VMEM((7, rows, width), BF16),
        pltpu.VMEM((2, rows, width), BF16),
        pltpu.VMEM((rows, width), BF16),
        pltpu.VMEM((2, part, feats // 2), F32),
        pltpu.VMEM((n_grp, part, width), BF16),
        pltpu.VMEM((rows, width), BF16),
        pltpu.VMEM((n_grp, part), F32),
        pltpu.VMEM((mates, n_grp, part), F32),
        pltpu.SemaphoreType.REGULAR,
        dma((mates,)), dma((mates,)),
        dma((7 * HALVES,)), dma((7, HALVES)),
        dma((hops - 1,)), dma((hops - 1,)),
        dma((mates,)), dma((mates,)),
        dma((hops,)), dma((hops,)),
        dma((hops, 2)), dma((hops, 2)),
        dma((7 * HALVES,)), dma((7, HALVES)),
        dma((mates,)), dma((mates,)),
        dma((mates,)), dma((mates,)),
    ]
    return pl.pallas_call(
        functools.partial(kernel, n_loop, n_grp),
        out_shape=jax.ShapeDtypeStruct((rows, width), F32),
        in_specs=[pl.BlockSpec(memory_space=pl.ANY)] * 2,
        out_specs=pl.BlockSpec(memory_space=pl.ANY),
        scratch_shapes=scratch,
        compiler_params=pltpu.CompilerParams(
            collective_id=0, has_side_effects=True, vmem_limit_bytes=56 * 2**20
        ),
        name="window_grad",
    )(student, teacher_tiles)


def solution(mesh):
    placed = (P("loop", "grp"), P(("loop", "grp"), None, None))
    return jax.shard_map(
        functools.partial(per_device, mesh.shape["loop"], mesh.shape["grp"]),
        mesh=mesh, in_specs=placed, out_specs=P("loop", "grp"), check_vma=False,
    )
```

```python
import functools

import jax
import jax.numpy as jnp
from jax import lax
from jax.experimental import pallas as pl
from jax.experimental.pallas import tpu as pltpu
from jax.sharding import PartitionSpec as P

MESH = pl.DeviceIdType.MESH
F32 = jnp.float32
BF16 = jnp.bfloat16
STEPS = 4
HALVES = 2
G_SIDE, G_LEFT, G_LEFT_SIDE, G_RIGHT, G_RIGHT_SIDE, G_LEFT_FAR, G_RIGHT_FAR = range(7)
R_LEFT_PASS, R_RIGHT_PASS, R_LEFT, R_RIGHT, R_LEFT_SUM, R_RIGHT_SUM, R_SIDE = range(7)


def to_lanes(column, eye):
    return jnp.sum(jnp.where(eye, column, 0.0), axis=0, keepdims=True)


def to_column(row, eye):
    return jnp.sum(jnp.where(eye, row, 0.0), axis=1, keepdims=True)


def kernel(
    n_loop, n_grp, s_hbm, t_hbm, out_hbm,
    s_ref, t_ref, out_ref, input_sem, output_sem,
    raw, unit, squares, norm, rows_raw, rows_norm, urows, sent_tiles, tiles, third, errors, errors_t, own_send, own_recv,
    far, landed, passed, side, own_total, own_rows, home_rows, inner_send, inner_recv,
    below_in, early_s, early_r, gather_s, gather_r, tile_s, tile_r, third_s, third_r, unit_s, unit_r, own_s, own_r, far_s, far_r,
    rows_s, rows_r, inner_s, inner_r,
):
    inputs = [
        pltpu.make_async_copy(s_hbm, s_ref, input_sem.at[0]),
        pltpu.make_async_copy(t_hbm, t_ref, input_sem.at[1]),
    ]
    for copy in inputs:
        copy.start()
    b = lax.axis_index("loop")
    g = lax.axis_index("grp")
    rows, width = s_ref.shape
    feats = width * n_grp
    part = rows // n_grp
    half = rows // HALVES
    step = half
    n_x = n_grp // 2
    x, y = lax.div(g, 2), lax.rem(g, 2)

    def at_x(dx, other=False):
        return lax.rem(x + dx + n_x, n_x) * 2 + (1 - y if other else y)

    def mate(d):
        return lax.rem(g + 1 + d, n_grp)

    def block(k):
        return (lax.rem(b + n_loop + k, n_loop), g)

    def part_of(h):
        return pl.ds(pl.multiple_of(h * part, part), part)

    def half_of(i):
        return pl.ds(i * half, half)

    def features(c):
        first = 1 - lax.div(g, n_grp // 2)
        return pl.ds(pl.multiple_of((first if c == 0 else 1 - first) * (feats // 2), feats // 2), feats // 2)

    started = []

    def send(src, dst, s, r, to):
        copy = pltpu.make_async_remote_copy(
            src_ref=src, dst_ref=dst, send_sem=s, recv_sem=r, device_id=to, device_id_type=MESH
        )
        copy.start()
        started.append(copy)
        return copy

    right, left, beside = (b, at_x(1)), (b, at_x(-1)), (b, at_x(0, True))

    barrier = pltpu.get_barrier_semaphore()
    for d in range(n_grp - 1):
        pl.semaphore_signal(barrier, inc=1, device_id=(b, mate(d)), device_id_type=MESH)
    for k in range(1, STEPS):
        pl.semaphore_signal(barrier, inc=1, device_id=block(-k), device_id_type=MESH)

    for copy in inputs:
        copy.wait()
    tiles[pl.ds(0, part), :] = t_ref[:, 0, :]
    for k in range(1, STEPS - 1):
        sent_tiles[k - 1] = t_ref[:, k, :]
    last = t_ref[:, STEPS - 1, :]
    for h in range(n_grp):
        third[0, h] = last[:, h * part : (h + 1) * part]
    raw[g] = s_ref[...]
    rows_raw[g] = s_ref[part_of(g), :]

    def add_squares(h, i, first=False):
        def piece(j, carry):
            at = pl.ds(pl.multiple_of(i * half + j * part, part), part)
            values = raw[h, at, :].astype(F32)
            squares[at, :] = values * values if first else squares[at, :] + values * values
            return carry

        lax.fori_loop(0, half // part, piece, 0)

    for i in range(HALVES):
        add_squares(g, i, first=True)

    pl.semaphore_wait(barrier, n_grp - 1 + STEPS - 1)
    for k in range(1, STEPS):
        pl.semaphore_signal(below_in, inc=1, device_id=block(k), device_id_type=MESH)

    early = [
        send(s_ref.at[part_of(mate(d)), :], rows_raw.at[g], early_s.at[d], early_r.at[d], (b, mate(d)))
        for d in range(n_grp - 1)
    ]
    sent_slices = []

    def give(h, i, slot, to, src=None):
        n = len(sent_slices)
        src = raw.at[h] if src is None else src
        sent_slices.append(
            send(src.at[half_of(i), :], raw.at[h, half_of(i), :], gather_s.at[n], gather_r.at[slot, i], to)
        )

    def take(slot, h, i):
        here = raw.at[h, half_of(i), :]
        pltpu.make_async_copy(here, here, gather_r.at[slot, i]).wait()

    for i in range(HALVES):
        give(g, i, G_SIDE, beside, s_ref)
        give(g, i, G_LEFT, right, s_ref)
        give(g, i, G_RIGHT, left, s_ref)

    def urow(k):
        return urows.at[pl.ds(k * part, part), :]

    third_copies = [
        send(third.at[0, mate(d)], third.at[1, g], third_s.at[d], third_r.at[d], (b, mate(d)))
        for d in range(n_grp - 1)
    ]
    def copy_to(src, dst, s, r, to):
        copy = pltpu.make_async_remote_copy(
            src_ref=src, dst_ref=dst, send_sem=s, recv_sem=r, device_id=to, device_id_type=MESH
        )
        started.append(copy)
        return copy

    def tile_copy(k):
        dst = tiles.at[pl.ds(k * part, part), :]
        return copy_to(sent_tiles.at[k - 1], dst, tile_s.at[k - 1], tile_r.at[k - 1], block(-k))

    tile_copies = [tile_copy(2), tile_copy(1)]
    wrap = lax.rem(b, n_loop // 2) < STEPS - 1

    @pl.when(jnp.logical_not(wrap))
    def _():
        pl.semaphore_wait(below_in, STEPS - 1)
        for copy in tile_copies:
            copy.start()

    third[1, g] = third[0, g]

    for copy in early:
        copy.wait_recv()
    total = jnp.zeros((part, width), F32)
    for h in range(n_grp):
        values = rows_raw[h].astype(F32)
        total = total + values * values
    norms = jnp.sqrt(jnp.sum(total, axis=1, keepdims=True) + 1e-06)
    rows_norm[...] = norms
    for h in range(n_grp):
        urows[0:part, h * width : (h + 1) * width] = (rows_raw[h].astype(F32) / norms).astype(BF16)

    unit_copies = [
        copy_to(urow(0), urow(1), unit_s.at[0], unit_r.at[0], block(-1)),
        copy_to(urow(0), urow(3), unit_s.at[2], unit_r.at[2], block(3)),
    ]
    unit_copies[1].start()

    @pl.when(jnp.logical_not(wrap))
    def _():
        unit_copies[0].start()

    def pass_on(i):
        take(G_SIDE, at_x(0, True), i)
        give(at_x(0, True), i, G_LEFT_SIDE, right)
        give(at_x(0, True), i, G_RIGHT_SIDE, left)
        take(G_LEFT, at_x(-1), i)
        give(at_x(-1), i, G_LEFT_FAR, right)

    def pass_back(i):
        take(G_RIGHT_SIDE, at_x(1, True), i)
        give(at_x(1, True), i, G_RIGHT_FAR, left)

    def use(i, *slices):
        for h in slices:
            add_squares(h, i)

    pass_on(0)
    pass_on(1)
    unit_copies.append(copy_to(urow(1), urow(2), unit_s.at[1], unit_r.at[1], block(-1)))

    def relay():
        unit_copies[0].wait_recv()
        unit_copies[2].start()

    @pl.when(jnp.logical_not(wrap))
    def _():
        relay()

    use(0, at_x(0, True), at_x(-1))
    pass_back(0)
    pass_back(1)
    @pl.when(wrap)
    def _():
        pl.semaphore_wait(below_in, STEPS - 1)
        unit_copies[0].start()
        for copy in tile_copies:
            copy.start()

    @pl.when(wrap)
    def _():
        relay()

    use(0, at_x(1, True))
    take(G_RIGHT, at_x(1), 0)
    take(G_LEFT_SIDE, at_x(-1, True), 0)
    use(0, at_x(1), at_x(-1, True))
    take(G_LEFT_FAR, at_x(-2), 0)
    use(0, at_x(-2))
    use(1, at_x(0, True), at_x(-1))
    for copy in third_copies:
        copy.wait_recv()
    for h in range(n_grp):
        tiles[3 * part : 4 * part, h * part : (h + 1) * part] = third[1, h].astype(F32).T.astype(BF16)
    take(G_RIGHT_FAR, at_x(2, True), 0)
    use(0, at_x(2, True))

    def normalise(i):
        def piece(j, carry):
            at = pl.ds(pl.multiple_of(i * half + j * part, part), part)
            norms = jnp.sqrt(jnp.sum(squares[at, :], axis=1, keepdims=True) + 1e-06)
            norm[at, :] = norms
            inverse = 1.0 / norms
            for h in range(n_grp):
                unit[at, h * width : (h + 1) * width] = (raw[h, at, :].astype(F32) * inverse).astype(BF16)
            return carry

        lax.fori_loop(0, half // part, piece, 0)

    def error_tiles(i):
        def piece(j, carry):
            at = pl.ds(pl.multiple_of(i * half + j * step, step), step)
            similar = lax.dot_general(
                urows[...], unit[at, :], (((1,), (1,)), ((), ())), preferred_element_type=F32
            )
            found = similar - tiles[:, at].astype(F32)
            errors[:, at] = found.astype(BF16)
            errors_t[at, :] = found.T.astype(BF16)
            return carry

        lax.fori_loop(0, half // step, piece, 0)

    def own_parts(c):
        found = jnp.dot(errors[...], unit[:, features(c)], preferred_element_type=F32)
        own_total[c] = found[:part]
        for k in range(1, STEPS):
            own_send[k - 1, c] = found[k * part : (k + 1) * part].astype(BF16)

    def far_pair(dx, i):
        pair = lax.rem(x + dx + n_x, n_x)
        mine = urows[:, pl.ds(pl.multiple_of(pair * 2 * width, 2 * width), 2 * width)]

        at = half_of(i)
        sums = jnp.dot(errors_t[at, :], mine, preferred_element_type=F32).astype(BF16)
        far[pair * 2, at, :] = sums[:, :width]
        far[pair * 2 + 1, at, :] = sums[:, width:]

    sent_sums = []

    def hand(src, i, slot, to):
        n = len(sent_sums)
        sent_sums.append(
            send(src.at[half_of(i), :], landed.at[slot, half_of(i), :], far_s.at[n], far_r.at[slot, i], to)
        )

    def got(slot, i):
        here = landed.at[slot, half_of(i), :]
        pltpu.make_async_copy(here, here, far_r.at[slot, i]).wait()

    def far_passes(i):
        far_pair(2, i)
        hand(far.at[at_x(2, True)], i, R_LEFT_PASS, right)
        hand(far.at[at_x(2)], i, R_RIGHT_PASS, left)

    def far_near(i):
        far_pair(-1, i)
        hand(far.at[at_x(-1, True)], i, R_RIGHT, left)
        far_pair(1, i)

    def add_left_pass(i):
        at = half_of(i)
        got(R_LEFT_PASS, i)
        passed[0, at, :] = (far[at_x(1, True), at, :].astype(F32) + landed[R_LEFT_PASS, at, :].astype(F32)).astype(BF16)
        hand(passed.at[0], i, R_LEFT_SUM, right)

    def add_right_pass(i):
        at = half_of(i)
        got(R_RIGHT_PASS, i)
        passed[1, at, :] = (far[at_x(-1), at, :].astype(F32) + landed[R_RIGHT_PASS, at, :].astype(F32)).astype(BF16)
        hand(passed.at[1], i, R_RIGHT_SUM, left)

    def add_side(i):
        at = half_of(i)
        got(R_RIGHT, i)
        got(R_LEFT_SUM, i)
        side[at, :] = (
            far[at_x(0, True), at, :].astype(F32)
            + landed[R_RIGHT, at, :].astype(F32)
            + landed[R_LEFT_SUM, at, :].astype(F32)
        ).astype(BF16)
        hand(side, i, R_SIDE, beside)

    for copy in tile_copies + unit_copies[1:]:
        copy.wait_recv()
    normalise(0)
    error_tiles(0)
    far_passes(0)
    far_near(0)
    hand(far.at[at_x(1)], 0, R_LEFT, right)

    use(1, at_x(1, True))
    take(G_RIGHT, at_x(1), 1)
    take(G_LEFT_SIDE, at_x(-1, True), 1)
    use(1, at_x(1), at_x(-1, True))
    take(G_LEFT_FAR, at_x(-2), 1)
    take(G_RIGHT_FAR, at_x(2, True), 1)
    use(1, at_x(-2), at_x(2, True))
    normalise(1)
    error_tiles(1)
    own_copies = []
    for c in range(2):
        own_parts(c)
        own_copies.append(
            [
                send(
                    own_send.at[k - 1, c],
                    own_recv.at[k - 1, c],
                    own_s.at[k - 1, c],
                    own_r.at[k - 1, c],
                    block(k if k < 3 else -3),
                )
                for k in range(1, STEPS)
            ]
        )
    far_passes(1)
    add_left_pass(0)
    add_right_pass(0)
    far_near(1)
    add_left_pass(1)
    hand(far.at[at_x(1)], 1, R_LEFT, right)
    add_right_pass(1)
    far_pair(0, 0)
    far_pair(0, 1)

    eye = lax.broadcasted_iota(jnp.int32, (part, part), 0) == lax.broadcasted_iota(jnp.int32, (part, part), 1)

    def inner_rows(i, carry):
        at = pl.ds(pl.multiple_of(i * part, part), part)
        dots = jnp.zeros((part, width), F32)
        for h in range(n_grp):
            dots = dots + raw[h, at, :].astype(F32) * far[h, at, :].astype(F32)
        inner_send[pl.ds(i, 1), :] = to_lanes(jnp.sum(dots, axis=1, keepdims=True) / norm[at, :], eye)
        return carry

    lax.fori_loop(0, n_grp, inner_rows, 0)
    add_side(0)

    dots = jnp.zeros((part, width), F32)
    rows_copies = []
    near = n_grp // 2
    mine = lax.div(g, near)
    for c in range(2):
        for copy in own_copies[c]:
            copy.wait_recv()
        total = own_total[c]
        for k in range(1, STEPS):
            total = total + own_recv[k - 1, c].astype(F32)
        group = 1 - mine if c == 0 else mine
        for i in range(near):
            h = group * near + i
            rounded = total[:, i * width : (i + 1) * width].astype(BF16)
            own_rows[h] = rounded
        for i in range(near - c):
            h = group * near + (i if c == 0 else lax.rem(g + 1 + i, near))
            slot = lax.rem(g - h - 1 + 2 * n_grp, n_grp)
            rows_copies.append(
                send(own_rows.at[h], home_rows.at[part_of(g), :], rows_s.at[len(rows_copies)], rows_r.at[slot], (b, h))
            )
    for h in range(n_grp):
        dots = dots + rows_raw[h].astype(F32) * own_rows[h].astype(F32)
    inner_send[pl.ds(g, 1), :] = inner_send[pl.ds(g, 1), :] + to_lanes(
        jnp.sum(dots, axis=1, keepdims=True) / rows_norm[...], eye
    )
    inner_copies = [
        send(inner_send, inner_recv.at[d], inner_s.at[d], inner_r.at[d], (b, mate(d))) for d in range(n_grp - 1)
    ]
    home_rows[part_of(g), :] = own_rows[g]

    add_side(1)

    def add_home(i):
        for slot in (R_LEFT, R_RIGHT_SUM, R_SIDE):
            got(slot, i)
        at = half_of(i)
        grad = far[g, at, :].astype(F32)
        for slot in (R_LEFT, R_RIGHT_SUM, R_SIDE):
            grad = grad + landed[slot, at, :].astype(F32)
        out_ref[at, :] = grad

    add_home(0)
    for copy in rows_copies + inner_copies:
        copy.wait_recv()
    inner = inner_send[...]
    for d in range(n_grp - 1):
        inner = inner + inner_recv[d]

    outputs = []
    for i in range(HALVES):
        if i > 0:
            add_home(i)
        for j in range(i * n_grp // HALVES, (i + 1) * n_grp // HALVES):
            at = pl.ds(j * part, part)
            grad = home_rows[at, :].astype(F32) + out_ref[at, :]
            inverse = 1.0 / norm[at, :]
            along = to_column(inner[j : j + 1, :], eye)
            out_ref[at, :] = (2.0 * inverse) * (grad - s_ref[at, :].astype(F32) * (inverse * along))
        outputs.append(
            pltpu.make_async_copy(out_ref.at[half_of(i), :], out_hbm.at[half_of(i), :], output_sem.at[i])
        )
        outputs[i].start()

    for copy in started:
        copy.wait_send()
    for copy in outputs:
        copy.wait()


def per_device(n_loop, n_grp, student, teacher_tiles):
    rows, width = student.shape
    feats = width * n_grp
    part = rows // n_grp
    mates, hops = n_grp - 1, STEPS - 1
    dma = pltpu.SemaphoreType.DMA
    scratch = [
        pltpu.VMEM((rows, width), BF16),
        pltpu.VMEM((part, STEPS, rows), BF16),
        pltpu.VMEM((rows, width), F32),
        dma((2,)),
        dma((HALVES,)),
        pltpu.VMEM((n_grp, rows, width), BF16),
        pltpu.VMEM((rows, feats), BF16),
        pltpu.VMEM((rows, width), F32),
        pltpu.VMEM((rows, 1), F32),
        pltpu.VMEM((n_grp, part, width), BF16),
        pltpu.VMEM((part, 1), F32),
        pltpu.VMEM((STEPS * part, feats), BF16),
        pltpu.VMEM((hops - 1, part, rows), BF16),
        pltpu.VMEM((STEPS * part, rows), BF16),
        pltpu.VMEM((2, n_grp, part, part), BF16),
        pltpu.VMEM((STEPS * part, rows), BF16),
        pltpu.VMEM((rows, STEPS * part), BF16),
        pltpu.VMEM((hops, 2, part, feats // 2), BF16),
        pltpu.VMEM((hops, 2, part, feats // 2), BF16),
        pltpu.VMEM((n_grp, rows, width), BF16),
        pltpu.VMEM((7, rows, width), BF16),
        pltpu.VMEM((2, rows, width), BF16),
        pltpu.VMEM((rows, width), BF16),
        pltpu.VMEM((2, part, feats // 2), F32),
        pltpu.VMEM((n_grp, part, width), BF16),
        pltpu.VMEM((rows, width), BF16),
        pltpu.VMEM((n_grp, part), F32),
        pltpu.VMEM((mates, n_grp, part), F32),
        pltpu.SemaphoreType.REGULAR,
        dma((mates,)), dma((mates,)),
        dma((7 * HALVES,)), dma((7, HALVES)),
        dma((hops - 1,)), dma((hops - 1,)),
        dma((mates,)), dma((mates,)),
        dma((hops,)), dma((hops,)),
        dma((hops, 2)), dma((hops, 2)),
        dma((7 * HALVES,)), dma((7, HALVES)),
        dma((mates,)), dma((mates,)),
        dma((mates,)), dma((mates,)),
    ]
    return pl.pallas_call(
        functools.partial(kernel, n_loop, n_grp),
        out_shape=jax.ShapeDtypeStruct((rows, width), F32),
        in_specs=[pl.BlockSpec(memory_space=pl.ANY)] * 2,
        out_specs=pl.BlockSpec(memory_space=pl.ANY),
        scratch_shapes=scratch,
        compiler_params=pltpu.CompilerParams(
            collective_id=0, has_side_effects=True, vmem_limit_bytes=56 * 2**20
        ),
        name="window_grad",
    )(student, teacher_tiles)


def solution(mesh):
    placed = (P("loop", "grp"), P(("loop", "grp"), None, None))
    return jax.shard_map(
        functools.partial(per_device, mesh.shape["loop"], mesh.shape["grp"]),
        mesh=mesh, in_specs=placed, out_specs=P("loop", "grp"), check_vma=False,
    )
```
